32 devices in a mesh: groups: 2 (over x), slab: 16 (over z, y, core).
Axes of the slice: x: 2, y: 2, z: 4, core: 2. Of those that a mesh axis runs over, the one named last changes fastest.
Arguments:
- features: bfloat16 [128, 16, 16, 128], P(('groups', 'slab')), parts along dimension 0, may hold values from -6 to 6
- filters_first: bfloat16 [3456, 128], P('slab'), may hold values from -0.109375 to 0.109375
- filters_second: bfloat16 [3456, 128], P('slab'), may hold values from -0.109375 to 0.109375
- cotangent: bfloat16 [128, 16, 16, 128], P(('groups', 'slab')), parts along dimension 0, may hold values from -0.125 to 0.125
Outputs:
- output: bfloat16 [128, 16, 16, 128], P(('groups', 'slab')), parts along dimension 0
- grad_first: float32 [6912, 128], P(('groups', 'slab')), parts along dimension 0
- grad_second: float32 [6912, 128], P(('groups', 'slab')), parts along dimension 0
The draws below stay inside these ranges and needn't reach their ends.
There are 2 independent parts, one for each index of `groups`. The reference program is written for one: setup_inputs(seed, part) draws one part's arguments, and reference() takes and returns one part's arrays. A program takes and returns all parts, laid end to end along the dimension named above; an argument that names none is the same for every part. Nothing has to cross between parts.
All inputs are finite; a program needn't handle non-finite values.
Results may differ from the reference program's by a relative error of at most 0.0049.
Values may be sent and summed in bfloat16 or wider, within the bound.
No kernel may reach another device: no remote copies, remote signals or barrier semaphores. Data moves between devices by JAX's collectives and lax.ppermute only.
A program may use at most 64 MiB of HBM per device.

```python
import jax
import jax.numpy as jnp
from jax import lax

C = 128
KTAPS = 27
PLANE_H = 16
PLANE_W = 16
NZ = 64
NCELLS = 16384


def levels(stream_key, extent, split, least, largest):
    gain, own = 1.0, jax.random.fold_in(stream_key, 6)
    for axis_at, parts in split:
        draws = jnp.exp(jax.random.uniform(jax.random.fold_in(own, axis_at), (parts,), jnp.float32, least / len(split), largest / len(split)))
        gain = gain * jnp.repeat(draws, extent[axis_at] // parts).reshape([-1 if axis == axis_at else 1 for axis in range(len(extent))])
    return gain


def bell_draw(key, dims, scale, reach, cuts=(), kind=jnp.bfloat16):
    values = scale * jax.random.normal(key, dims, jnp.float32)
    if cuts:
        values = values * levels(key, dims, cuts, -0.22, 0.18)
    return jnp.clip(values, -reach, reach).astype(kind)


def setup_inputs(seed: int = 0, part: int = 0) -> dict:
    keys = jax.random.split(jax.random.key(seed), 5)
    part_splits = jax.random.split(jax.random.fold_in(keys[4], part), 5)
    features = bell_draw(part_splits[0], (NZ, PLANE_H, PLANE_W, C), 1.0, 6.0, ((0, 16),))
    filters_first = bell_draw(keys[1], (KTAPS * C, C), (KTAPS * C) ** -0.5, 0.109375, ((0, 16),))
    filters_second = bell_draw(keys[2], (KTAPS * C, C), (KTAPS * C) ** -0.5, 0.109375, ((0, 16),))
    cotangent = bell_draw(part_splits[3], (NZ, PLANE_H, PLANE_W, C), (NCELLS ** -0.5), 0.125, ((0, 16),))
    return {"features": features, "filters_first": filters_first, "filters_second": filters_second, "cotangent": cotangent}


inv_root_two = 0.7071067811865476
inv_root_two_pi = 0.3989422804014327

def shifted(padded, offset_z, offset_y, offset_x, shape):
    piece = padded[offset_z:offset_z + shape[0], offset_y:offset_y + shape[1], offset_x:offset_x + shape[2], :]
    return piece.reshape(-1, shape[3])

def forward_conv(padded, weight, shape):
    channels = shape[3]
    total = jnp.zeros((shape[0] * shape[1] * shape[2], channels), jnp.float32)
    for offset_z in range(3):
        for offset_y in range(3):
            for offset_x in range(3):
                tap = (offset_z * 3 + offset_y) * 3 + offset_x
                block = weight[tap * channels:(tap + 1) * channels]
                total = total + jnp.dot(shifted(padded, offset_z, offset_y, offset_x, shape), block, preferred_element_type=jnp.float32)
    return total.reshape(shape)

def transpose_conv(padded, weight, shape):
    channels = shape[3]
    total = jnp.zeros((shape[0] * shape[1] * shape[2], channels), jnp.float32)
    for offset_z in range(3):
        for offset_y in range(3):
            for offset_x in range(3):
                tap = (offset_z * 3 + offset_y) * 3 + offset_x
                block = weight[tap * channels:(tap + 1) * channels]
                piece = shifted(padded, 2 - offset_z, 2 - offset_y, 2 - offset_x, shape)
                total = total + lax.dot_general(piece, block, (((1,), (1,)), ((), ())), preferred_element_type=jnp.float32)
    return total.reshape(shape)

def weight_grad(padded, gradient, shape):
    flat = gradient.reshape(-1, shape[3])
    blocks = []
    for offset_z in range(3):
        for offset_y in range(3):
            for offset_x in range(3):
                piece = shifted(padded, offset_z, offset_y, offset_x, shape)
                blocks.append(lax.dot_general(piece, flat, (((0,), (0,)), ((), ())), preferred_element_type=jnp.float32))
    return jnp.concatenate(blocks, axis=0)

def gelu_parts(value):
    normal_cdf = 0.5 * (1.0 + lax.erf(value * inv_root_two))
    slope = normal_cdf + value * jnp.exp(-0.5 * value * value) * inv_root_two_pi
    return (value * normal_cdf, slope)

def pad_all(value):
    return jnp.pad(value, ((1, 1), (1, 1), (1, 1), (0, 0)))

def reference(features, filters_first, filters_second, cotangent):
    shape = features.shape
    padded_input = pad_all(features)
    pre = forward_conv(padded_input, filters_first, shape)
    active, slope = gelu_parts(pre)
    hidden = active.astype(jnp.bfloat16)
    padded_hidden = pad_all(hidden)
    output = forward_conv(padded_hidden, filters_second, shape).astype(jnp.bfloat16)
    padded_grad = pad_all(cotangent)
    grad_hidden = transpose_conv(padded_grad, filters_second, shape)
    grad_pre = (grad_hidden * slope).astype(jnp.bfloat16)
    grad_second = weight_grad(padded_hidden, cotangent, shape)
    grad_first = weight_grad(padded_input, grad_pre, shape)
    return (output, grad_first, grad_second)
```

```python
import functools

import jax
import jax.numpy as jnp
from jax import lax
from jax.experimental import pallas as pl
from jax.experimental.pallas import tpu as pltpu
from jax.sharding import PartitionSpec as P

inv_root_two = 0.7071067811865476
inv_root_two_pi = 0.3989422804014327

BF16 = jnp.bfloat16
F32 = jnp.float32
MIB = 1 << 20


def gelu_parts(value):
    normal_cdf = 0.5 * (1.0 + lax.erf(value * inv_root_two))
    slope = normal_cdf + value * jnp.exp(-0.5 * value * value) * inv_root_two_pi
    return (value * normal_cdf, slope)


def local_call(kernel, name, outs, args, scratch=(), flops=0, limit=24 * MIB, scalars=0):
    moved = sum(a.size * a.dtype.itemsize for a in args)
    moved += sum(o.size * o.dtype.itemsize for o in outs)
    specs = [
        pl.BlockSpec(memory_space=pltpu.SMEM if at < scalars else pltpu.VMEM)
        for at in range(len(args))
    ]
    return pl.pallas_call(
        kernel,
        out_shape=list(outs),
        in_specs=specs,
        out_specs=[pl.BlockSpec(memory_space=pltpu.VMEM) for _ in outs],
        scratch_shapes=list(scratch),
        name=name,
        compiler_params=pltpu.CompilerParams(vmem_limit_bytes=limit),
        cost_estimate=pl.CostEstimate(flops=flops, bytes_accessed=moved, transcendentals=0),
    )(*args)


def like(shape, dtype):
    return jax.ShapeDtypeStruct(shape, dtype)


def write_shifted(dst, at, plane):
    height, width, channels = plane.shape
    flat = plane.astype(F32).reshape(height * width, channels)
    column = lax.broadcasted_iota(jnp.int32, flat.shape, 0) % width
    left = jnp.where(column == 0, 0.0, pltpu.roll(flat, 1, 0))
    right = jnp.where(column == width - 1, 0.0, pltpu.roll(flat, height * width - 1, 0))
    row = jnp.zeros((1, width, 3 * channels), BF16)
    dst[at, 0:1] = row
    dst[at, height + 1 : height + 2] = row
    for block, value in enumerate((left, flat, right)):
        dst[at, 1 : height + 1, :, block * channels : (block + 1) * channels] = (
            value.astype(BF16).reshape(height, width, channels)
        )


def prepare_kernel(f_ref, g_ref, lo_ref, hi_ref, xf_ref, xg_ref, xt_ref):
    planes, height, width, channels = f_ref.shape
    for p in range(2):
        write_shifted(xf_ref, p, lo_ref[p])
        write_shifted(xf_ref, planes + 2 + p, hi_ref[p])
    write_shifted(xg_ref, 0, lo_ref[2])
    write_shifted(xg_ref, planes + 1, hi_ref[2])
    for p in range(planes):
        write_shifted(xf_ref, p + 2, f_ref[p])
        write_shifted(xg_ref, p + 1, g_ref[p])

    def transposed(p, _):
        for b in range(3):
            for c in range(3):
                window = xf_ref[p + 1, b : b + height, :, c * channels : (c + 1) * channels]
                xt_ref[p, b * 3 + c] = window.reshape(height * width, channels).T
        return 0

    lax.fori_loop(0, planes + 2, transposed, 0)


def window(ref, first, planes):
    height, width, lanes = ref.shape[1] - 2, ref.shape[2], ref.shape[3]
    return jnp.concatenate(
        [
            ref[first : first + planes, b : b + height].reshape(planes * height * width, lanes)
            for b in range(3)
        ],
        axis=1,
    )


def conv_rows(ref, first, planes, weight_ref):
    depth = weight_ref.shape[0] // 3
    total = None
    for a in range(3):
        term = jnp.dot(
            window(ref, first + a, planes),
            weight_ref[a * depth : (a + 1) * depth],
            preferred_element_type=F32,
        )
        total = term if total is None else total + term
    return total


def assemble(me, pieces, dst):
    rows = pieces[0].shape[1]
    for low, piece in enumerate(pieces):
        for d in range(piece.shape[0]):
            start = pl.multiple_of((me ^ (4 * d + low)) * rows, 8)
            dst[pl.ds(start, rows)] = piece[d]


def split_terms(me, total_ref, send_ref, keep_ref):
    count, rows, _ = keep_ref.shape
    core = me % 2
    for k in range(count):
        own = pl.multiple_of((2 * k + core) * rows, 8)
        other = pl.multiple_of((2 * k + 1 - core) * rows, 8)
        keep_ref[k] = total_ref[pl.ds(own, rows)]
        send_ref[k] = total_ref[pl.ds(other, rows)].astype(BF16)


def first_kernel(
    me_ref, w0, w1, w2, w3, xf_ref, xg_ref, bank_ref, hidden_ref, slope_ref, send_ref, keep_ref, total_ref
):
    me = me_ref[0]
    planes, height, width, channels = hidden_ref.shape
    assemble(me, (w0, w1, w2, w3), bank_ref)
    pre = conv_rows(xf_ref, 1, planes, bank_ref)
    active, slope = gelu_parts(pre)
    slope_ref[...] = slope
    hidden = active.astype(BF16)
    hidden_ref[...] = hidden.reshape(hidden_ref.shape)
    flipped = hidden.T
    for a in range(3):
        out = jnp.dot(flipped, window(xg_ref, 2 - a, planes), preferred_element_type=F32)
        for b in range(3):
            for c in range(3):
                tap = (a * 3 + b) * 3 + c
                source = (2 - b) * 3 + 2 - c
                total_ref[tap * channels : (tap + 1) * channels] = out[
                    :, source * channels : (source + 1) * channels
                ]
    split_terms(me, total_ref, send_ref, keep_ref)


def second_kernel(
    me_ref, w0, w1, w2, w3, xg_ref, xt_ref, slope_ref, bank_ref, send_ref, keep_ref, back_ref, total_ref
):
    me = me_ref[0]
    channels = slope_ref.shape[1]
    planes = xg_ref.shape[0] - 2
    cells = slope_ref.shape[0] // planes
    assemble(me, (w0, w1, w2, w3), bank_ref)
    for tap in range(27):
        a, rest = divmod(tap, 9)
        to = (2 - a) * 9 + 8 - rest
        back_ref[to * channels : (to + 1) * channels] = bank_ref[
            tap * channels : (tap + 1) * channels
        ].T
    grad_hidden = conv_rows(xg_ref, 0, planes, back_ref)
    grad_pre = (grad_hidden * slope_ref[...]).astype(BF16)
    depth = 9 * channels
    for a in range(3):
        total = None
        for z in range(planes):
            term = jnp.dot(
                xt_ref[z + a].reshape(depth, cells),
                grad_pre[z * cells : (z + 1) * cells],
                preferred_element_type=F32,
            )
            total = term if total is None else total + term
        total_ref[a * depth : (a + 1) * depth] = total
    split_terms(me, total_ref, send_ref, keep_ref)


def output_kernel(me_ref, count, xf_ref, bank_ref, hidden_ref, second_ref, out_ref, xh_ref):
    me = me_ref[0]
    planes, height, width, channels = hidden_ref.shape
    for at, first, inside in ((0, 0, me > 0), (planes + 1, planes + 1, me < count - 1)):
        active, _ = gelu_parts(conv_rows(xf_ref, first, 1, bank_ref))
        active = jnp.where(inside, active, 0.0)
        write_shifted(xh_ref, at, active.astype(BF16).reshape(height, width, channels))
    for p in range(planes):
        write_shifted(xh_ref, p + 1, hidden_ref[p])
    out = conv_rows(xh_ref, 0, planes, second_ref)
    out_ref[...] = out.astype(BF16).reshape(out_ref.shape)


def sum_pair_kernel(me_ref, keep_ref, got_ref, send_ref, own_ref):
    half = (me_ref[0] // 2) % 2
    for d in range(own_ref.shape[0]):
        own_ref[d] = keep_ref[2 * d + half] + got_ref[2 * d + half].astype(F32)
        other = 2 * d + 1 - half
        send_ref[d] = (keep_ref[other] + got_ref[other].astype(F32)).astype(BF16)


def sum_rows_kernel(me_ref, keep_ref, got_ref, own_ref, *send_refs):
    at = me_ref[0] // 4
    own_ref[...] = keep_ref[at] + got_ref[at].astype(F32)
    for d, send_ref in enumerate(send_refs, 1):
        send_ref[...] = (keep_ref[at ^ d] + got_ref[at ^ d].astype(F32)).astype(BF16)


def sum_last_kernel(keep_ref, *refs):
    total = keep_ref[...]
    for ref in refs[:-1]:
        total = total + ref[...].astype(F32)
    refs[-1][...] = total


def swap(value, count, distance):
    return lax.ppermute(value, "slab", [(i, i ^ distance) for i in range(count)])


def gather_bank(shard, count):
    own = jnp.stack([shard] + [swap(shard, count, 4 * d) for d in range(1, count // 4)])
    across = swap(own, count, 2)
    return own, swap(own, count, 1), across, swap(across, count, 1)


def scatter_terms(me, send, keep, count, rows, channels, name):
    groups = count // 4
    got = swap(send, count, 1)
    send, keep = local_call(
        sum_pair_kernel,
        name + "_pair",
        [like((groups, rows, channels), BF16), like((groups, rows, channels), F32)],
        [me, keep, got],
        scalars=1,
    )
    got = swap(send, count, 2)
    own, *sends = local_call(
        sum_rows_kernel,
        name + "_rows",
        [like((rows, channels), F32)] + [like((rows, channels), BF16)] * (groups - 1),
        [me, keep, got],
        scalars=1,
    )
    gots = [swap(value, count, 4 * d) for d, value in enumerate(sends, 1)]
    (total,) = local_call(
        sum_last_kernel, name + "_last", [like((rows, channels), F32)], [own, *gots]
    )
    return total


def shards(count, features, filters_first, filters_second, cotangent):
    planes, height, width, channels = features.shape
    cells = planes * height * width
    rows = filters_first.shape[0]
    taps = 27 * channels
    direct = count in (8, 16) and rows % 8 == 0
    me = lax.axis_index("slab").astype(jnp.int32).reshape(1)
    up = [(i, i + 1) for i in range(count - 1)]
    down = [(i + 1, i) for i in range(count - 1)]
    low = lax.ppermute(jnp.concatenate([features[-2:], cotangent[-1:]]), "slab", up)
    high = lax.ppermute(jnp.concatenate([features[:2], cotangent[:1]]), "slab", down)
    if direct:
        first = gather_bank(filters_first, count)
        second = gather_bank(filters_second, count)
        shard_rows = rows
    else:
        shard_rows = taps // 16
        first = whole_pieces(filters_first, shard_rows)
        second = whole_pieces(filters_second, shard_rows)
    place = me if direct else jnp.zeros((1,), jnp.int32)
    kept = taps // shard_rows // 2

    xf, xg, xt = local_call(
        prepare_kernel,
        "shifted_planes",
        [
            like((planes + 4, height + 2, width, 3 * channels), BF16),
            like((planes + 2, height + 2, width, 3 * channels), BF16),
            like((planes + 2, 9, channels, height * width), BF16),
        ],
        [features, cotangent, low, high],
    )
    flops = 2 * cells * taps * channels
    bank, hidden, slope, send_second, keep_second = local_call(
        first_kernel,
        "hidden_and_second_grad",
        [
            like((taps, channels), BF16),
            like(features.shape, BF16),
            like((cells, channels), F32),
            like((kept, shard_rows, channels), BF16),
            like((kept, shard_rows, channels), F32),
        ],
        [place, *first, xf, xg],
        scratch=[pltpu.VMEM((taps, channels), F32)],
        flops=2 * flops,
        scalars=1,
    )
    bank_second, send_first, keep_first = local_call(
        second_kernel,
        "first_grad",
        [
            like((taps, channels), BF16),
            like((kept, shard_rows, channels), BF16),
            like((kept, shard_rows, channels), F32),
        ],
        [place, *second, xg, xt, slope],
        scratch=[pltpu.VMEM((taps, channels), BF16), pltpu.VMEM((taps, channels), F32)],
        flops=2 * flops,
        scalars=1,
    )
    (output,) = local_call(
        lambda me_ref, *refs: output_kernel(me_ref, count, *refs),
        "output_conv",
        [like(features.shape, BF16)],
        [me, xf, bank, hidden, bank_second],
        scratch=[pltpu.VMEM((planes + 2, height + 2, width, 3 * channels), BF16)],
        flops=flops,
        scalars=1,
    )
    if direct:
        grads = [
            scatter_terms(me, send, keep, count, rows, channels, name)
            for send, keep, name in (
                (send_second, keep_second, "second"),
                (send_first, keep_first, "first"),
            )
        ]
    else:
        grads = [
            lax.psum_scatter(
                jnp.stack([keep, send.astype(F32)], 1).reshape(taps, channels),
                "slab",
                scatter_dimension=0,
                tiled=True,
            )
            for send, keep in ((send_second, keep_second), (send_first, keep_first))
        ]
    return (output, grads[1], grads[0])


def whole_pieces(shard, shard_rows):
    bank = lax.all_gather(shard, "slab", axis=0, tiled=True)
    parts = bank.reshape(-1, 4, shard_rows, bank.shape[1])
    return tuple(parts[:, low] for low in range(4))


def solution(mesh):
    return jax.shard_map(
        functools.partial(shards, mesh.shape["slab"]),
        mesh=mesh,
        in_specs=(
            P(("groups", "slab"), None, None, None),
            P("slab", None),
            P("slab", None),
            P(("groups", "slab"), None, None, None),
        ),
        out_specs=(
            P(("groups", "slab"), None, None, None),
            P(("groups", "slab"), None),
            P(("groups", "slab"), None),
        ),
        check_vma=False,
    )
```

```python
import functools

import jax
import jax.numpy as jnp
from jax import lax
from jax.experimental import pallas as pl
from jax.experimental.pallas import tpu as pltpu
from jax.sharding import PartitionSpec as P

inv_root_two = 0.7071067811865476
inv_root_two_pi = 0.3989422804014327

BF16 = jnp.bfloat16
F32 = jnp.float32
LIMIT = 14 << 20


def gelu_parts(value):
    normal_cdf = 0.5 * (1.0 + lax.erf(value * inv_root_two))
    slope = normal_cdf + value * jnp.exp(-0.5 * value * value) * inv_root_two_pi
    return (value * normal_cdf, slope)


def local_call(kernel, name, outs, args, scratch=(), scalars=0, wait_for=()):
    first, last = len(args), len(args) + len(wait_for)

    def body(*refs):
        kernel(*refs[:first], *refs[last:])

    spaces = [pltpu.SMEM] * scalars + [pltpu.VMEM] * (first - scalars) + [pl.ANY] * len(wait_for)
    return pl.pallas_call(
        body,
        out_shape=list(outs),
        in_specs=[pl.BlockSpec(memory_space=space) for space in spaces],
        out_specs=[pl.BlockSpec(memory_space=pltpu.VMEM) for _ in outs],
        scratch_shapes=list(scratch),
        name=name,
        compiler_params=pltpu.CompilerParams(vmem_limit_bytes=LIMIT),
        cost_estimate=pl.CostEstimate(flops=1000, bytes_accessed=0, transcendentals=0),
    )(*args, *wait_for)


def like(shape, dtype):
    return jax.ShapeDtypeStruct(shape, dtype)


def write_shifted(dst, at, plane):
    height, width, channels = plane.shape
    flat = plane.astype(F32).reshape(height * width, channels)
    column = lax.broadcasted_iota(jnp.int32, flat.shape, 0) % width
    left = jnp.where(column == 0, 0.0, pltpu.roll(flat, 1, 0))
    right = jnp.where(column == width - 1, 0.0, pltpu.roll(flat, height * width - 1, 0))
    row = jnp.zeros((1, width, 3 * channels), BF16)
    dst[at, 0:1] = row
    dst[at, height + 1 : height + 2] = row
    for block, value in enumerate((left, flat, right)):
        dst[at, 1 : height + 1, :, block * channels : (block + 1) * channels] = (
            value.astype(BF16).reshape(height, width, channels)
        )


def prepare_kernel(me_ref, f_ref, g_ref, core_ref, chip_ref, xf_ref, xg_ref, gt_ref):
    planes, height, width, channels = f_ref.shape
    odd = me_ref[0] % 2
    for ref, below in ((core_ref, odd), (chip_ref, 1 - odd)):
        for p in range(2):
            write_shifted(xf_ref, jnp.where(below == 1, p, planes + 2 + p), ref[p])
        write_shifted(xg_ref, jnp.where(below == 1, 0, planes + 1), ref[2])
    for p in range(planes):
        write_shifted(xf_ref, p + 2, f_ref[p])
        write_shifted(xg_ref, p + 1, g_ref[p])

    def transposed(p, _):
        for b in range(3):
            for c in range(3):
                block = xg_ref[p, b : b + height, :, c * channels : (c + 1) * channels]
                gt_ref[p, b * 3 + c] = block.reshape(height * width, channels).T
        return 0

    lax.fori_loop(0, planes + 2, transposed, 0)


def load_kernel(f_hbm, g_hbm, first_hbm, second_hbm, *refs):
    f_ref, g_ref, first_ref, second_ref, sems = refs
    moves = [
        pltpu.make_async_copy(source, target, sems.at[at])
        for at, (source, target) in enumerate(
            (
                (first_hbm, first_ref.at[0]),
                (second_hbm, second_ref.at[0]),
                (f_hbm, f_ref),
                (g_hbm, g_ref),
            )
        )
    ]
    for move in moves:
        move.start()
    for move in moves:
        move.wait()


def edges_kernel(me_ref, f_ref, g_ref, core_ref, chip_ref):
    planes = f_ref.shape[0]
    odd = me_ref[0] % 2
    for ref, low in ((core_ref, odd == 1), (chip_ref, odd == 0)):
        ref[0:2] = f_ref[pl.ds(jnp.where(low, 0, planes - 2), 2)]
        ref[2:3] = g_ref[pl.ds(jnp.where(low, 0, planes - 1), 1)]


def loaded(features, first, second, cotangent):
    args = [
        pltpu.with_memory_space_constraint(a, pltpu.HBM)
        for a in (features, cotangent, first, second)
    ]
    return pl.pallas_call(
        load_kernel,
        out_shape=[
            like(features.shape, BF16),
            like(cotangent.shape, BF16),
            like((1, *first.shape), BF16),
            like((1, *second.shape), BF16),
        ],
        in_specs=[pl.BlockSpec(memory_space=pltpu.HBM) for _ in args],
        out_specs=[pl.BlockSpec(memory_space=pltpu.VMEM) for _ in range(4)],
        scratch_shapes=[pltpu.SemaphoreType.DMA((len(args),))],
        name="load",
        compiler_params=pltpu.CompilerParams(vmem_limit_bytes=LIMIT),
    )(*args)


def join_kernel(*refs):
    *parts, out_ref = refs
    at = 0
    for part in parts:
        if len(part.shape) == 2:
            out_ref[at] = part[...]
            at += 1
        else:
            out_ref[at : at + part.shape[0]] = part[...]
            at += part.shape[0]


def window(ref, first, planes):
    height, width, lanes = ref.shape[1] - 2, ref.shape[2], ref.shape[3]
    return jnp.concatenate(
        [
            ref[first : first + planes, b : b + height].reshape(planes * height * width, lanes)
            for b in range(3)
        ],
        axis=1,
    )


def conv_rows(ref, first, planes, weight_ref):
    depth = weight_ref.shape[0] // 3
    cells = (ref.shape[1] - 2) * ref.shape[2]
    taps = [weight_ref[a * depth : (a + 1) * depth] for a in range(3)]

    def term(at, count, weight):
        return jnp.dot(window(ref, first + at, count), weight, preferred_element_type=F32)

    if planes == 1:
        return sum(term(a, 1, taps[a]) for a in range(3))
    channels = taps[0].shape[1]
    middle = term(1, planes - 1, jnp.concatenate(taps[:2], axis=1))
    late = term(2, planes - 2, taps[2])
    ends = (term(0, 1, taps[0]), term(planes + 1, 1, taps[2]))
    last = term(planes, 1, jnp.concatenate(taps[1:], axis=1))
    parts = [[] for _ in range(planes)]
    parts[0].append(ends[0])
    for p in range(1, planes):
        rows = slice((p - 1) * cells, p * cells)
        parts[p].append(middle[rows, :channels])
        parts[p - 1].append(middle[rows, channels:])
    for p in range(2, planes):
        parts[p - 2].append(late[(p - 2) * cells : (p - 1) * cells])
    parts[planes - 1].append(last[:, :channels])
    parts[planes - 2].append(last[:, channels:])
    parts[planes - 1].append(ends[1])
    return jnp.concatenate([sum(terms[1:], terms[0]) for terms in parts], axis=0)


def near_far(core):
    return jnp.where(core == 0, 4, 2), jnp.where(core == 0, 2, 4)


def assemble(me, pieces, dst):
    rows = pieces[0].shape[1]
    near, far = near_far(me % 2)
    for piece, start, side in zip(
        pieces, (me, me ^ far, me ^ 1, me ^ 1 ^ near), (near, near, far, far)
    ):
        for at, owner in enumerate((start, start ^ 8, start ^ side, start ^ 8 ^ side)):
            dst[pl.ds(pl.multiple_of(owner * rows, 8), rows)] = piece[at]


def assemble_in_order(me, pieces, dst):
    dst[...] = pieces[0][...]


def split_terms(me, total_ref, send_ref, keep_ref):
    count, rows, _ = keep_ref.shape
    core = me % 2
    for k in range(count):
        own = pl.multiple_of((2 * k + core) * rows, 8)
        other = pl.multiple_of((2 * k + 1 - core) * rows, 8)
        keep_ref[k] = total_ref[pl.ds(own, rows)]
        send_ref[k] = total_ref[pl.ds(other, rows)].astype(BF16)


def first_kernel(pieces, place, me_ref, *refs):
    piece_refs, (xf_ref, xg_ref, *out_refs) = refs[:pieces], refs[pieces:]
    bank_ref, hidden_ref, slope_ref, send_ref, keep_ref, total_ref = out_refs
    me = me_ref[0]
    planes, height, width, channels = hidden_ref.shape
    place(me, piece_refs, bank_ref)
    active, slope = gelu_parts(conv_rows(xf_ref, 1, planes, bank_ref))
    slope_ref[...] = slope.T
    hidden = active.astype(BF16)
    hidden_ref[...] = hidden.reshape(hidden_ref.shape)
    flipped = hidden.T
    for a in range(3):
        out = jnp.dot(flipped, window(xg_ref, 2 - a, planes), preferred_element_type=F32)
        for rest in range(9):
            tap, source = a * 9 + rest, 8 - rest
            total_ref[tap * channels : (tap + 1) * channels] = out[
                :, source * channels : (source + 1) * channels
            ]
    split_terms(me, total_ref, send_ref, keep_ref)


def second_kernel(pieces, place, me_ref, *refs):
    piece_refs, (xf_ref, gt_ref, slope_ref, *out_refs) = refs[:pieces], refs[pieces:]
    bank_ref, send_ref, keep_ref, total_ref = out_refs
    me = me_ref[0]
    channels = slope_ref.shape[0]
    planes, _, _, cells = gt_ref.shape
    planes -= 2
    place(me, piece_refs, bank_ref)
    back = jnp.concatenate(
        [bank_ref[tap * channels : (tap + 1) * channels] for tap in reversed(range(27))], axis=1
    )
    grads = []
    for z in range(planes):
        grad_hidden = jnp.dot(
            back, gt_ref[z : z + 3].reshape(27 * channels, cells), preferred_element_type=F32
        )
        grads.append((grad_hidden * slope_ref[:, z * cells : (z + 1) * cells]).astype(BF16))
    grad_pre = jnp.concatenate(grads, axis=1)
    for a in range(3):
        out = jnp.dot(grad_pre, window(xf_ref, 1 + a, planes), preferred_element_type=F32)
        for rest in range(9):
            tap = a * 9 + rest
            total_ref[tap * channels : (tap + 1) * channels] = out[
                :, rest * channels : (rest + 1) * channels
            ].T
    split_terms(me, total_ref, send_ref, keep_ref)


def hidden_kernel(count, me_ref, xf_ref, bank_ref, hidden_ref, xh_ref):
    me = me_ref[0]
    planes, height, width, channels = hidden_ref.shape
    for at, first, inside in ((0, 0, me > 0), (planes + 1, planes + 1, me < count - 1)):
        active, _ = gelu_parts(conv_rows(xf_ref, first, 1, bank_ref))
        active = jnp.where(inside, active, 0.0)
        write_shifted(xh_ref, at, active.astype(BF16).reshape(height, width, channels))
    for p in range(planes):
        write_shifted(xh_ref, p + 1, hidden_ref[p])


def output_kernel(xh_ref, second_ref, out_ref):
    out = conv_rows(xh_ref, 0, out_ref.shape[0], second_ref)
    out_ref[...] = out.astype(BF16).reshape(out_ref.shape)


def sum_half(bit, place, keep_ref, got_ref, send_ref, own_ref):
    for at in range(own_ref.shape[0]):
        mine, other = place(at, bit), place(at, 1 - bit)
        own_ref[at] = keep_ref[mine] + got_ref[mine].astype(F32)
        send_ref[at] = (keep_ref[other] + got_ref[other].astype(F32)).astype(BF16)


def sum_pair_kernel(me_ref, *refs):
    me = me_ref[0]
    core = me % 2
    bit = jnp.where(core == 0, (me // 2) % 2, (me // 4) % 2)

    def place(at, value):
        return jnp.where(core == 0, 2 * at + value, at // 2 * 4 + 2 * value + at % 2)

    sum_half(bit, place, *refs)


def sum_near_kernel(me_ref, *refs):
    me = me_ref[0]
    bit = jnp.where(me % 2 == 0, (me // 4) % 2, (me // 2) % 2)
    sum_half(bit, lambda at, value: 2 * at + value, *refs)


def sum_far_kernel(me_ref, *refs):
    sum_half(me_ref[0] // 8, lambda at, value: value, *refs)


def sum_last_kernel(keep_first, got_first, keep_second, got_second, first_ref, second_ref):
    first_ref[...] = keep_first[0] + got_first[0].astype(F32)
    second_ref[...] = keep_second[0] + got_second[0].astype(F32)


def swap(value, count, distance):
    return lax.ppermute(value, "slab", [(i, i ^ distance) for i in range(count)])


def swap_mixed(value, count, even, odd):
    pairs = [(i, i ^ (odd if i % 2 else even)) for i in range(count)]
    return lax.ppermute(value, "slab", pairs)


def joined(parts, name, wait_for=()):
    depth = sum(part.shape[0] if part.ndim == 3 else 1 for part in parts)
    out = like((depth, *parts[0].shape[-2:]), BF16)
    return local_call(join_kernel, name, [out], parts, wait_for=wait_for)[0]


def summed(kernel, name, me, keep, got, wait_for=()):
    shape = (keep.shape[0] // 2, *keep.shape[1:])
    outs = [like(shape, BF16), like(shape, F32)]
    return local_call(kernel, name, outs, [me, keep, got], scalars=1, wait_for=wait_for)


def shards(count, features, filters_first, filters_second, cotangent):
    planes, height, width, channels = features.shape
    cells = planes * height * width
    rows = filters_first.shape[0]
    taps = 27 * channels
    direct = count == 16 and rows % 8 == 0
    me = lax.axis_index("slab").astype(jnp.int32).reshape(1)
    shard_rows = rows if direct else taps // 16
    place = me if direct else jnp.zeros((1,), jnp.int32)
    order = assemble if direct else assemble_in_order

    features, cotangent, first_shard, second_shard = loaded(
        features, filters_first, filters_second, cotangent
    )
    edge = like((3, height, width, channels), BF16)
    to_core, to_chip = local_call(
        edges_kernel, "edges", [edge, edge], [me, features, cotangent], scalars=1
    )
    from_core = swap(to_core, count, 1)
    next_chip = [(i, i + 1 if i % 2 else i - 1) for i in range(1, count - 1)]
    from_chip = lax.ppermute(to_chip, "slab", next_chip)
    xf, xg, gt = local_call(
        prepare_kernel,
        "shifted_planes",
        [
            like((planes + 4, height + 2, width, 3 * channels), BF16),
            like((planes + 2, height + 2, width, 3 * channels), BF16),
            like((planes + 2, 9, channels, height * width), BF16),
        ],
        [me, features, cotangent, from_core, from_chip],
        scalars=1,
    )
    wait_for = []
    if direct:
        far = [swap(shard, count, 8) for shard in (filters_first, filters_second)]
        two_first = joined([first_shard, far[0]], "first_two", [from_chip])
        near_first = swap_mixed(two_first, count, 4, 2)
        two_second = joined([second_shard, far[1]], "second_two")
        near_second = swap_mixed(two_second, count, 4, 2)
        four_first = joined([two_first, near_first], "first_four", [two_second, xf])
        cross_first = swap_mixed(four_first, count, 2, 4)
        four_second = joined([two_second, near_second], "second_four")
        cross_second = swap_mixed(four_second, count, 2, 4)
        wait_for = [cross_second]
        first = [four_first, cross_first, swap(four_first, count, 1), swap(cross_first, count, 1)]
        second = [
            four_second,
            cross_second,
            swap(four_second, count, 1),
            swap(cross_second, count, 1),
        ]
    else:
        first, second = (
            [lax.all_gather(shard, "slab", axis=0, tiled=True)]
            for shard in (filters_first, filters_second)
        )

    terms = [like((8, shard_rows, channels), BF16), like((8, shard_rows, channels), F32)]
    total = pltpu.VMEM((taps, channels), F32)
    bank, hidden, slope, send_second, keep_second = local_call(
        functools.partial(first_kernel, len(first), order),
        "hidden_and_second_grad",
        [
            like((taps, channels), BF16),
            like(features.shape, BF16),
            like((channels, cells), F32),
            *terms,
        ],
        [place, *first, xf, xg],
        scratch=[total],
        scalars=1,
        wait_for=wait_for,
    )
    bank_second, send_first, keep_first = local_call(
        functools.partial(second_kernel, len(second), order),
        "first_grad",
        [like((taps, channels), BF16), *terms],
        [place, *second, xf, gt, slope],
        scratch=[total],
        scalars=1,
    )
    wait_for = []
    if direct:
        got = swap(send_second, count, 1)
        send_second, keep_second = summed(sum_pair_kernel, "second_pair", me, keep_second, got)
        got_second = swap_mixed(send_second, count, 2, 4)
        got = swap(send_first, count, 1)
    (xh,) = local_call(
        functools.partial(hidden_kernel, count),
        "hidden_planes",
        [like((planes + 2, height + 2, width, 3 * channels), BF16)],
        [me, xf, bank, hidden],
        scalars=1,
        wait_for=[keep_first],
    )
    if direct:
        send_first, keep_first = summed(sum_pair_kernel, "first_pair", me, keep_first, got, [xh])
        got_first = swap_mixed(send_first, count, 2, 4)
        send_second, keep_second = summed(
            sum_near_kernel, "second_near", me, keep_second, got_second, [send_first]
        )
        got_second = swap_mixed(send_second, count, 4, 2)
        send_first, keep_first = summed(
            sum_near_kernel, "first_near", me, keep_first, got_first, [send_second]
        )
        got_first = swap_mixed(send_first, count, 4, 2)
        send_second, keep_second = summed(
            sum_far_kernel, "second_far", me, keep_second, got_second, [send_first]
        )
        got_second = swap(send_second, count, 8)
        send_first, keep_first = summed(
            sum_far_kernel, "first_far", me, keep_first, got_first, [send_second]
        )
        wait_for = [send_first]
    (output,) = local_call(
        output_kernel, "output_conv", [like(features.shape, BF16)], [xh, bank_second], wait_for=wait_for
    )
    if direct:
        out = like((rows, channels), F32)
        grad_first, grad_second = local_call(
            sum_last_kernel,
            "sum_last",
            [out, out],
            [keep_first, swap(send_first, count, 8), keep_second, got_second],
        )
    else:
        grad_first, grad_second = (
            lax.psum_scatter(
                jnp.stack([keep, send.astype(F32)], 1).reshape(taps, channels),
                "slab",
                scatter_dimension=0,
                tiled=True,
            )
            for send, keep in ((send_first, keep_first), (send_second, keep_second))
        )
    return (output, grad_first, grad_second)


def solution(mesh):
    return jax.shard_map(
        functools.partial(shards, mesh.shape["slab"]),
        mesh=mesh,
        in_specs=(
            P(("groups", "slab"), None, None, None),
            P("slab", None),
            P("slab", None),
            P(("groups", "slab"), None, None, None),
        ),
        out_specs=(
            P(("groups", "slab"), None, None, None),
            P(("groups", "slab"), None),
            P(("groups", "slab"), None),
        ),
        check_vma=False,
    )
```

```python
import functools

import jax
import jax.numpy as jnp
from jax import lax
from jax.experimental import pallas as pl
from jax.experimental.pallas import tpu as pltpu
from jax.sharding import PartitionSpec as P

inv_root_two = 0.7071067811865476
inv_root_two_pi = 0.3989422804014327

BF16 = jnp.bfloat16
F32 = jnp.float32
LIMIT = 14 << 20


def gelu_parts(value):
    normal_cdf = 0.5 * (1.0 + lax.erf(value * inv_root_two))
    slope = normal_cdf + value * jnp.exp(-0.5 * value * value) * inv_root_two_pi
    return (value * normal_cdf, slope)


def local_call(kernel, name, outs, args, scratch=(), scalars=0, wait_for=()):
    first, last = len(args), len(args) + len(wait_for)

    def body(*refs):
        kernel(*refs[:first], *refs[last:])

    spaces = [pltpu.SMEM] * scalars + [pltpu.VMEM] * (first - scalars) + [pl.ANY] * len(wait_for)
    return pl.pallas_call(
        body,
        out_shape=list(outs),
        in_specs=[pl.BlockSpec(memory_space=space) for space in spaces],
        out_specs=[pl.BlockSpec(memory_space=pltpu.VMEM) for _ in outs],
        scratch_shapes=list(scratch),
        name=name,
        compiler_params=pltpu.CompilerParams(vmem_limit_bytes=LIMIT),
        cost_estimate=pl.CostEstimate(flops=1000, bytes_accessed=0, transcendentals=0),
    )(*args, *wait_for)


def like(shape, dtype):
    return jax.ShapeDtypeStruct(shape, dtype)


def write_shifted(dst, at, plane):
    height, width, channels = plane.shape
    flat = plane.astype(F32).reshape(height * width, channels)
    column = lax.broadcasted_iota(jnp.int32, flat.shape, 0) % width
    left = jnp.where(column == 0, 0.0, pltpu.roll(flat, 1, 0))
    right = jnp.where(column == width - 1, 0.0, pltpu.roll(flat, height * width - 1, 0))
    row = jnp.zeros((1, width, 3 * channels), BF16)
    dst[at, 0:1] = row
    dst[at, height + 1 : height + 2] = row
    for block, value in enumerate((left, flat, right)):
        dst[at, 1 : height + 1, :, block * channels : (block + 1) * channels] = (
            value.astype(BF16).reshape(height, width, channels)
        )


def prepare_kernel(me_ref, f_ref, g_ref, core_ref, chip_ref, xf_ref, xg_ref, gt_ref):
    planes, height, width, channels = f_ref.shape
    odd = me_ref[0] % 2
    for ref, below in ((core_ref, odd), (chip_ref, 1 - odd)):
        for p in range(2):
            write_shifted(xf_ref, jnp.where(below == 1, p, planes + 2 + p), ref[p])
        write_shifted(xg_ref, jnp.where(below == 1, 0, planes + 1), ref[2])
    for p in range(planes):
        write_shifted(xf_ref, p + 2, f_ref[p])
        write_shifted(xg_ref, p + 1, g_ref[p])

    def transposed(p, _):
        for b in range(3):
            for c in range(3):
                block = xg_ref[p, b : b + height, :, c * channels : (c + 1) * channels]
                gt_ref[p, b * 3 + c] = block.reshape(height * width, channels).T
        return 0

    lax.fori_loop(0, planes + 2, transposed, 0)


def copy_all(moves, sems):
    copies = [
        pltpu.make_async_copy(source, target, sems.at[at])
        for at, (source, target) in enumerate(moves)
    ]
    for copy in copies:
        copy.start()
    for copy in copies:
        copy.wait()


def load_kernel(f_hbm, g_hbm, f_ref, g_ref, sems):
    copy_all(((f_hbm, f_ref), (g_hbm, g_ref)), sems)


def load_shards_kernel(first_hbm, second_hbm, shards_ref, sems):
    copy_all(((first_hbm, shards_ref.at[0]), (second_hbm, shards_ref.at[1])), sems)


def edges_kernel(me_ref, f_hbm, g_hbm, core_ref, chip_ref, sems):
    planes = f_hbm.shape[0]
    odd = me_ref[0] % 2
    moves = []
    for ref, low in ((chip_ref, odd == 0), (core_ref, odd == 1)):
        moves.append((f_hbm.at[pl.ds(jnp.where(low, 0, planes - 2), 2)], ref.at[pl.ds(0, 2)]))
        moves.append((g_hbm.at[pl.ds(jnp.where(low, 0, planes - 1), 1)], ref.at[pl.ds(2, 1)]))
    copy_all(moves, sems)


def from_hbm(kernel, name, outs, args, scalars=(), wait_for=()):
    args = [pltpu.with_memory_space_constraint(a, pltpu.HBM) for a in args]
    first, last = len(scalars) + len(args), len(scalars) + len(args) + len(wait_for)

    def body(*refs):
        kernel(*refs[:first], *refs[last:])

    spaces = [pltpu.SMEM] * len(scalars) + [pltpu.HBM] * len(args) + [pl.ANY] * len(wait_for)
    return pl.pallas_call(
        body,
        out_shape=outs,
        in_specs=[pl.BlockSpec(memory_space=space) for space in spaces],
        out_specs=[pl.BlockSpec(memory_space=pltpu.VMEM) for _ in outs],
        scratch_shapes=[pltpu.SemaphoreType.DMA((4,))],
        name=name,
        compiler_params=pltpu.CompilerParams(vmem_limit_bytes=LIMIT),
        cost_estimate=pl.CostEstimate(flops=1000, bytes_accessed=0, transcendentals=0),
    )(*scalars, *args, *wait_for)


def join_kernel(*refs):
    *parts, out_ref = refs
    at = 0
    for part in parts:
        if len(part.shape) == 2:
            out_ref[at] = part[...]
            at += 1
        else:
            out_ref[at : at + part.shape[0]] = part[...]
            at += part.shape[0]


def window(ref, first, planes):
    height, width, lanes = ref.shape[1] - 2, ref.shape[2], ref.shape[3]
    return jnp.concatenate(
        [
            ref[first : first + planes, b : b + height].reshape(planes * height * width, lanes)
            for b in range(3)
        ],
        axis=1,
    )


def conv_rows(ref, first, planes, weight_ref):
    depth = weight_ref.shape[0] // 3
    cells = (ref.shape[1] - 2) * ref.shape[2]
    taps = [weight_ref[a * depth : (a + 1) * depth] for a in range(3)]

    def term(at, count, weight):
        return jnp.dot(window(ref, first + at, count), weight, preferred_element_type=F32)

    if planes == 1:
        return sum(term(a, 1, taps[a]) for a in range(3))
    channels = taps[0].shape[1]
    middle = term(1, planes - 1, jnp.concatenate(taps[:2], axis=1))
    late = term(2, planes - 2, taps[2])
    ends = (term(0, 1, taps[0]), term(planes + 1, 1, taps[2]))
    last = term(planes, 1, jnp.concatenate(taps[1:], axis=1))
    parts = [[] for _ in range(planes)]
    parts[0].append(ends[0])
    for p in range(1, planes):
        rows = slice((p - 1) * cells, p * cells)
        parts[p].append(middle[rows, :channels])
        parts[p - 1].append(middle[rows, channels:])
    for p in range(2, planes):
        parts[p - 2].append(late[(p - 2) * cells : (p - 1) * cells])
    parts[planes - 1].append(last[:, :channels])
    parts[planes - 2].append(last[:, channels:])
    parts[planes - 1].append(ends[1])
    return jnp.concatenate([sum(terms[1:], terms[0]) for terms in parts], axis=0)


def near_far(core):
    return jnp.where(core == 0, 4, 2), jnp.where(core == 0, 2, 4)


def assemble(bank, me, pieces, dst):
    rows = pieces[0].shape[1]
    near, far = near_far(me % 2)
    starts = (me, me ^ 8, me ^ far, me ^ 8 ^ far)
    starts += tuple(start ^ 1 for start in (me, me ^ 8, me ^ near, me ^ 8 ^ near))
    for at, (piece, start) in enumerate(zip(pieces, starts)):
        for next_to, owner in enumerate((start, start ^ (near if at < 4 else far))):
            dst[pl.ds(pl.multiple_of(owner * rows, 8), rows)] = piece[2 * next_to + bank]


def assemble_in_order(bank, me, pieces, dst):
    dst[...] = pieces[bank][...]


def split_terms(me, total_ref, send_ref, keep_ref):
    count, rows, _ = keep_ref.shape
    core = me % 2
    for k in range(count):
        own = pl.multiple_of((2 * k + core) * rows, 8)
        other = pl.multiple_of((2 * k + 1 - core) * rows, 8)
        keep_ref[k] = total_ref[pl.ds(own, rows)]
        send_ref[k] = total_ref[pl.ds(other, rows)].astype(BF16)


def first_kernel(pieces, place, me_ref, *refs):
    piece_refs, (xf_ref, xg_ref, *out_refs) = refs[:pieces], refs[pieces:]
    bank_ref, hidden_ref, slope_ref, send_ref, keep_ref, total_ref = out_refs
    me = me_ref[0]
    planes, height, width, channels = hidden_ref.shape
    place(0, me, piece_refs, bank_ref)
    active, slope = gelu_parts(conv_rows(xf_ref, 1, planes, bank_ref))
    slope_ref[...] = slope.T
    hidden = active.astype(BF16)
    hidden_ref[...] = hidden.reshape(hidden_ref.shape)
    flipped = hidden.T
    for a in range(3):
        out = jnp.dot(flipped, window(xg_ref, 2 - a, planes), preferred_element_type=F32)
        for rest in range(9):
            tap, source = a * 9 + rest, 8 - rest
            total_ref[tap * channels : (tap + 1) * channels] = out[
                :, source * channels : (source + 1) * channels
            ]
    split_terms(me, total_ref, send_ref, keep_ref)


def second_kernel(pieces, place, me_ref, *refs):
    piece_refs, (xf_ref, gt_ref, slope_ref, *out_refs) = refs[:pieces], refs[pieces:]
    bank_ref, send_ref, keep_ref, total_ref = out_refs
    me = me_ref[0]
    channels = slope_ref.shape[0]
    planes, _, _, cells = gt_ref.shape
    planes -= 2
    place(1, me, piece_refs, bank_ref)
    back = jnp.concatenate(
        [bank_ref[tap * channels : (tap + 1) * channels] for tap in reversed(range(27))], axis=1
    )
    grads = []
    for z in range(planes):
        grad_hidden = jnp.dot(
            back, gt_ref[z : z + 3].reshape(27 * channels, cells), preferred_element_type=F32
        )
        grads.append((grad_hidden * slope_ref[:, z * cells : (z + 1) * cells]).astype(BF16))
    grad_pre = jnp.concatenate(grads, axis=1)
    for a in range(3):
        out = jnp.dot(grad_pre, window(xf_ref, 1 + a, planes), preferred_element_type=F32)
        for rest in range(9):
            tap = a * 9 + rest
            total_ref[tap * channels : (tap + 1) * channels] = out[
                :, rest * channels : (rest + 1) * channels
            ].T
    split_terms(me, total_ref, send_ref, keep_ref)


def hidden_kernel(count, me_ref, xf_ref, bank_ref, hidden_ref, xh_ref):
    me = me_ref[0]
    planes, height, width, channels = hidden_ref.shape
    for at, first, inside in ((0, 0, me > 0), (planes + 1, planes + 1, me < count - 1)):
        active, _ = gelu_parts(conv_rows(xf_ref, first, 1, bank_ref))
        active = jnp.where(inside, active, 0.0)
        write_shifted(xh_ref, at, active.astype(BF16).reshape(height, width, channels))
    for p in range(planes):
        write_shifted(xh_ref, p + 1, hidden_ref[p])


def output_kernel(xh_ref, second_ref, out_ref):
    out = conv_rows(xh_ref, 0, out_ref.shape[0], second_ref)
    out_ref[...] = out.astype(BF16).reshape(out_ref.shape)


def sum_half(bit, place, keep_ref, got_ref, send_ref, own_ref):
    for at in range(own_ref.shape[0]):
        mine, other = place(at, bit), place(at, 1 - bit)
        own_ref[at] = keep_ref[mine] + got_ref[mine].astype(F32)
        send_ref[at] = (keep_ref[other] + got_ref[other].astype(F32)).astype(BF16)


def sum_pair_kernel(me_ref, *refs):
    me = me_ref[0]
    core = me % 2
    bit = jnp.where(core == 0, (me // 2) % 2, (me // 4) % 2)

    def place(at, value):
        return jnp.where(core == 0, 2 * at + value, at // 2 * 4 + 2 * value + at % 2)

    sum_half(bit, place, *refs)


def sum_near_kernel(me_ref, *refs):
    me = me_ref[0]
    bit = jnp.where(me % 2 == 0, (me // 4) % 2, (me // 2) % 2)
    sum_half(bit, lambda at, value: 2 * at + value, *refs)


def sum_far_kernel(me_ref, *refs):
    sum_half(me_ref[0] // 8, lambda at, value: value, *refs)


def sum_last_kernel(keep_first, got_first, keep_second, got_second, first_ref, second_ref):
    first_ref[...] = keep_first[0] + got_first[0].astype(F32)
    second_ref[...] = keep_second[0] + got_second[0].astype(F32)


def swap(value, count, distance):
    return lax.ppermute(value, "slab", [(i, i ^ distance) for i in range(count)])


def swap_mixed(value, count, even, odd):
    pairs = [(i, i ^ (odd if i % 2 else even)) for i in range(count)]
    return lax.ppermute(value, "slab", pairs)


def joined(parts, name, wait_for=()):
    depth = sum(part.shape[0] if part.ndim == 3 else 1 for part in parts)
    out = like((depth, *parts[0].shape[-2:]), BF16)
    return local_call(join_kernel, name, [out], parts, wait_for=wait_for)[0]


def summed(kernel, name, me, keep, got, wait_for=()):
    shape = (keep.shape[0] // 2, *keep.shape[1:])
    outs = [like(shape, BF16), like(shape, F32)]
    return local_call(kernel, name, outs, [me, keep, got], scalars=1, wait_for=wait_for)


def shards(count, features, filters_first, filters_second, cotangent):
    planes, height, width, channels = features.shape
    cells = planes * height * width
    rows = filters_first.shape[0]
    taps = 27 * channels
    direct = count == 16 and rows % 8 == 0
    me = lax.axis_index("slab").astype(jnp.int32).reshape(1)
    shard_rows = rows if direct else taps // 16
    place = me if direct else jnp.zeros((1,), jnp.int32)
    order = assemble if direct else assemble_in_order

    edge = like((3, height, width, channels), BF16)
    to_core, to_chip = from_hbm(edges_kernel, "edges", [edge, edge], [features, cotangent], [me])
    (own,) = from_hbm(
        load_shards_kernel,
        "load_shards",
        [like((2, rows, channels), BF16)],
        [filters_first, filters_second],
    )
    features, cotangent = from_hbm(
        load_kernel,
        "load",
        [like(features.shape, BF16), like(cotangent.shape, BF16)],
        [features, cotangent],
        wait_for=[to_chip],
    )
    from_core = swap(to_core, count, 1)
    next_chip = [(i, i + 1 if i % 2 else i - 1) for i in range(1, count - 1)]
    from_chip = lax.ppermute(to_chip, "slab", next_chip)
    xf, xg, gt = local_call(
        prepare_kernel,
        "shifted_planes",
        [
            like((planes + 4, height + 2, width, 3 * channels), BF16),
            like((planes + 2, height + 2, width, 3 * channels), BF16),
            like((planes + 2, 9, channels, height * width), BF16),
        ],
        [me, features, cotangent, from_core, from_chip],
        scalars=1,
    )
    wait_for = []
    if direct:
        far = swap(own, count, 8)
        near = swap_mixed(own, count, 4, 2)
        close = joined([own, near], "own_and_near", [])
        cross = swap_mixed(close, count, 2, 4)
        near = swap_mixed(far, count, 4, 2)
        away = joined([far, near], "far_and_near", [xf])
        cross_away = swap_mixed(away, count, 2, 4)
        pieces = [close, away, cross, cross_away]
        pieces += [swap(piece, count, 1) for piece in pieces]
    else:
        pieces = [
            lax.all_gather(shard, "slab", axis=0, tiled=True)
            for shard in (filters_first, filters_second)
        ]
    terms = [like((8, shard_rows, channels), BF16), like((8, shard_rows, channels), F32)]
    total = pltpu.VMEM((taps, channels), F32)
    bank, hidden, slope, send_second, keep_second = local_call(
        functools.partial(first_kernel, len(pieces), order),
        "hidden_and_second_grad",
        [
            like((taps, channels), BF16),
            like(features.shape, BF16),
            like((channels, cells), F32),
            *terms,
        ],
        [place, *pieces, xf, xg],
        scratch=[total],
        scalars=1,
        wait_for=wait_for,
    )
    bank_second, send_first, keep_first = local_call(
        functools.partial(second_kernel, len(pieces), order),
        "first_grad",
        [like((taps, channels), BF16), *terms],
        [place, *pieces, xf, gt, slope],
        scratch=[total],
        scalars=1,
    )
    wait_for = []
    if direct:
        got = swap(send_second, count, 1)
        send_second, keep_second = summed(sum_pair_kernel, "second_pair", me, keep_second, got)
        got_second = swap_mixed(send_second, count, 2, 4)
        got = swap(send_first, count, 1)
    (xh,) = local_call(
        functools.partial(hidden_kernel, count),
        "hidden_planes",
        [like((planes + 2, height + 2, width, 3 * channels), BF16)],
        [me, xf, bank, hidden],
        scalars=1,
        wait_for=[keep_first],
    )
    if direct:
        send_first, keep_first = summed(sum_pair_kernel, "first_pair", me, keep_first, got, [xh])
        got_first = swap_mixed(send_first, count, 2, 4)
        send_second, keep_second = summed(
            sum_near_kernel, "second_near", me, keep_second, got_second, [send_first]
        )
        got_second = swap_mixed(send_second, count, 4, 2)
        send_first, keep_first = summed(
            sum_near_kernel, "first_near", me, keep_first, got_first, [send_second]
        )
        got_first = swap_mixed(send_first, count, 4, 2)
        send_second, keep_second = summed(
            sum_far_kernel, "second_far", me, keep_second, got_second, [send_first]
        )
        got_second = swap(send_second, count, 8)
        send_first, keep_first = summed(
            sum_far_kernel, "first_far", me, keep_first, got_first, [send_second]
        )
        wait_for = [send_first]
    (output,) = local_call(
        output_kernel, "output_conv", [like(features.shape, BF16)], [xh, bank_second], wait_for=wait_for
    )
    if direct:
        out = like((rows, channels), F32)
        grad_first, grad_second = local_call(
            sum_last_kernel,
            "sum_last",
            [out, out],
            [keep_first, swap(send_first, count, 8), keep_second, got_second],
        )
    else:
        grad_first, grad_second = (
            lax.psum_scatter(
                jnp.stack([keep, send.astype(F32)], 1).reshape(taps, channels),
                "slab",
                scatter_dimension=0,
                tiled=True,
            )
            for send, keep in ((send_first, keep_first), (send_second, keep_second))
        )
    return (output, grad_first, grad_second)


def solution(mesh):
    return jax.shard_map(
        functools.partial(shards, mesh.shape["slab"]),
        mesh=mesh,
        in_specs=(
            P(("groups", "slab"), None, None, None),
            P("slab", None),
            P("slab", None),
            P(("groups", "slab"), None, None, None),
        ),
        out_specs=(
            P(("groups", "slab"), None, None, None),
            P(("groups", "slab"), None),
            P(("groups", "slab"), None),
        ),
        check_vma=False,
    )
```

```python
import functools

import jax
import jax.numpy as jnp
from jax import lax
from jax.experimental import pallas as pl
from jax.experimental.pallas import tpu as pltpu
from jax.sharding import PartitionSpec as P

inv_root_two = 0.7071067811865476
inv_root_two_pi = 0.3989422804014327

BF16 = jnp.bfloat16
F32 = jnp.float32
LIMIT = 14 << 20


def gelu_parts(value):
    normal_cdf = 0.5 * (1.0 + lax.erf(value * inv_root_two))
    slope = normal_cdf + value * jnp.exp(-0.5 * value * value) * inv_root_two_pi
    return (value * normal_cdf, slope)


def local_call(kernel, name, outs, args, scratch=(), scalars=0, wait_for=()):
    first, last = len(args), len(args) + len(wait_for)

    def body(*refs):
        kernel(*refs[:first], *refs[last:])

    spaces = [pltpu.SMEM] * scalars + [pltpu.VMEM] * (first - scalars) + [pl.ANY] * len(wait_for)
    return pl.pallas_call(
        body,
        out_shape=list(outs),
        in_specs=[pl.BlockSpec(memory_space=space) for space in spaces],
        out_specs=[pl.BlockSpec(memory_space=pltpu.VMEM) for _ in outs],
        scratch_shapes=list(scratch),
        name=name,
        compiler_params=pltpu.CompilerParams(vmem_limit_bytes=LIMIT),
        cost_estimate=pl.CostEstimate(flops=1000, bytes_accessed=0, transcendentals=0),
    )(*args, *wait_for)


def like(shape, dtype):
    return jax.ShapeDtypeStruct(shape, dtype)


def write_shifted(dst, at, plane):
    height, width, channels = plane.shape
    flat = plane.astype(F32).reshape(height * width, channels)
    column = lax.broadcasted_iota(jnp.int32, flat.shape, 0) % width
    left = jnp.where(column == 0, 0.0, pltpu.roll(flat, 1, 0))
    right = jnp.where(column == width - 1, 0.0, pltpu.roll(flat, height * width - 1, 0))
    row = jnp.zeros((1, width, 3 * channels), BF16)
    dst[at, 0:1] = row
    dst[at, height + 1 : height + 2] = row
    for block, value in enumerate((left, flat, right)):
        dst[at, 1 : height + 1, :, block * channels : (block + 1) * channels] = (
            value.astype(BF16).reshape(height, width, channels)
        )


def prepare_kernel(me_ref, f_ref, g_ref, core_ref, chip_ref, xf_ref, xg_ref, gt_ref):
    planes, height, width, channels = f_ref.shape
    odd = me_ref[0] % 2
    for ref, below in ((core_ref, odd), (chip_ref, 1 - odd)):
        for p in range(2):
            write_shifted(xf_ref, jnp.where(below == 1, p, planes + 2 + p), ref[p])
        write_shifted(xg_ref, jnp.where(below == 1, 0, planes + 1), ref[2])
    for p in range(planes):
        write_shifted(xf_ref, p + 2, f_ref[p])
        write_shifted(xg_ref, p + 1, g_ref[p])

    def transposed(p, _):
        for b in range(3):
            for c in range(3):
                block = xg_ref[p, b : b + height, :, c * channels : (c + 1) * channels]
                gt_ref[p, b * 3 + c] = block.reshape(height * width, channels).T
        return 0

    lax.fori_loop(0, planes + 2, transposed, 0)


def copy_all(moves, sems):
    copies = [
        pltpu.make_async_copy(source, target, sems.at[at])
        for at, (source, target) in enumerate(moves)
    ]
    for copy in copies:
        copy.start()
    for copy in copies:
        copy.wait()


def load_kernel(f_hbm, g_hbm, f_ref, g_ref, sems):
    copy_all(((f_hbm, f_ref), (g_hbm, g_ref)), sems)


def load_shards_kernel(first_hbm, second_hbm, shards_ref, sems):
    copy_all(((first_hbm, shards_ref.at[0]), (second_hbm, shards_ref.at[1])), sems)


def edges_kernel(me_ref, f_hbm, g_hbm, core_ref, chip_ref, sems):
    planes = f_hbm.shape[0]
    odd = me_ref[0] % 2
    moves = []
    for ref, low in ((chip_ref, odd == 0), (core_ref, odd == 1)):
        moves.append((f_hbm.at[pl.ds(jnp.where(low, 0, planes - 2), 2)], ref.at[pl.ds(0, 2)]))
        moves.append((g_hbm.at[pl.ds(jnp.where(low, 0, planes - 1), 1)], ref.at[pl.ds(2, 1)]))
    copy_all(moves, sems)


def from_hbm(kernel, name, outs, args, scalars=(), wait_for=()):
    args = [pltpu.with_memory_space_constraint(a, pltpu.HBM) for a in args]
    first, last = len(scalars) + len(args), len(scalars) + len(args) + len(wait_for)

    def body(*refs):
        kernel(*refs[:first], *refs[last:])

    spaces = [pltpu.SMEM] * len(scalars) + [pltpu.HBM] * len(args) + [pl.ANY] * len(wait_for)
    return pl.pallas_call(
        body,
        out_shape=outs,
        in_specs=[pl.BlockSpec(memory_space=space) for space in spaces],
        out_specs=[pl.BlockSpec(memory_space=pltpu.VMEM) for _ in outs],
        scratch_shapes=[pltpu.SemaphoreType.DMA((4,))],
        name=name,
        compiler_params=pltpu.CompilerParams(vmem_limit_bytes=LIMIT),
        cost_estimate=pl.CostEstimate(flops=1000, bytes_accessed=0, transcendentals=0),
    )(*scalars, *args, *wait_for)


def join_kernel(*refs):
    *parts, out_ref = refs
    at = 0
    for part in parts:
        if len(part.shape) == 2:
            out_ref[at] = part[...]
            at += 1
        else:
            out_ref[at : at + part.shape[0]] = part[...]
            at += part.shape[0]


def window(ref, first, planes):
    height, width, lanes = ref.shape[1] - 2, ref.shape[2], ref.shape[3]
    return jnp.concatenate(
        [
            ref[first : first + planes, b : b + height].reshape(planes * height * width, lanes)
            for b in range(3)
        ],
        axis=1,
    )


def conv_rows(ref, first, planes, weight_ref):
    depth = weight_ref.shape[0] // 3
    cells = (ref.shape[1] - 2) * ref.shape[2]
    taps = [weight_ref[a * depth : (a + 1) * depth] for a in range(3)]

    def term(at, count, weight):
        return jnp.dot(window(ref, first + at, count), weight, preferred_element_type=F32)

    if planes == 1:
        return sum(term(a, 1, taps[a]) for a in range(3))
    channels = taps[0].shape[1]
    middle = term(1, planes - 1, jnp.concatenate(taps[:2], axis=1))
    late = term(2, planes - 2, taps[2])
    ends = (term(0, 1, taps[0]), term(planes + 1, 1, taps[2]))
    last = term(planes, 1, jnp.concatenate(taps[1:], axis=1))
    parts = [[] for _ in range(planes)]
    parts[0].append(ends[0])
    for p in range(1, planes):
        rows = slice((p - 1) * cells, p * cells)
        parts[p].append(middle[rows, :channels])
        parts[p - 1].append(middle[rows, channels:])
    for p in range(2, planes):
        parts[p - 2].append(late[(p - 2) * cells : (p - 1) * cells])
    parts[planes - 1].append(last[:, :channels])
    parts[planes - 2].append(last[:, channels:])
    parts[planes - 1].append(ends[1])
    return jnp.concatenate([sum(terms[1:], terms[0]) for terms in parts], axis=0)


def near_far(core):
    return jnp.where(core == 0, 4, 2), jnp.where(core == 0, 2, 4)


def assemble(bank, me, pieces, dst):
    rows = pieces[0].shape[1]
    near, far = near_far(me % 2)
    starts = (me, me ^ 8, me ^ far, me ^ 8 ^ far)
    starts += tuple(start ^ 1 for start in (me, me ^ 8, me ^ near, me ^ 8 ^ near))
    for at, (piece, start) in enumerate(zip(pieces, starts)):
        for next_to, owner in enumerate((start, start ^ (near if at < 4 else far))):
            dst[pl.ds(pl.multiple_of(owner * rows, 8), rows)] = piece[2 * next_to + bank]


def assemble_in_order(bank, me, pieces, dst):
    dst[...] = pieces[bank][...]


def split_terms(me, total_ref, send_ref, keep_ref):
    count, rows, _ = keep_ref.shape
    core = me % 2
    for k in range(count):
        own = pl.multiple_of((2 * k + core) * rows, 8)
        other = pl.multiple_of((2 * k + 1 - core) * rows, 8)
        keep_ref[k] = total_ref[pl.ds(own, rows)]
        send_ref[k] = total_ref[pl.ds(other, rows)].astype(BF16)


def first_kernel(pieces, place, me_ref, *refs):
    piece_refs, (xf_ref, xg_ref, *out_refs) = refs[:pieces], refs[pieces:]
    bank_ref, hidden_ref, slope_ref, send_ref, keep_ref, total_ref = out_refs
    me = me_ref[0]
    planes, height, width, channels = hidden_ref.shape
    place(0, me, piece_refs, bank_ref)
    active, slope = gelu_parts(conv_rows(xf_ref, 1, planes, bank_ref))
    slope_ref[...] = slope.T
    hidden = active.astype(BF16)
    hidden_ref[...] = hidden.reshape(hidden_ref.shape)
    flipped = hidden.T
    for a in range(3):
        out = jnp.dot(flipped, window(xg_ref, 2 - a, planes), preferred_element_type=F32)
        for rest in range(9):
            tap, source = a * 9 + rest, 8 - rest
            total_ref[tap * channels : (tap + 1) * channels] = out[
                :, source * channels : (source + 1) * channels
            ]
    split_terms(me, total_ref, send_ref, keep_ref)


def second_kernel(pieces, place, me_ref, *refs):
    piece_refs, (xf_ref, gt_ref, slope_ref, *out_refs) = refs[:pieces], refs[pieces:]
    bank_ref, send_ref, keep_ref, total_ref = out_refs
    me = me_ref[0]
    channels = slope_ref.shape[0]
    planes, _, _, cells = gt_ref.shape
    planes -= 2
    place(1, me, piece_refs, bank_ref)
    back = jnp.concatenate(
        [bank_ref[tap * channels : (tap + 1) * channels] for tap in reversed(range(27))], axis=1
    )
    grads = []
    for z in range(planes):
        grad_hidden = jnp.dot(
            back, gt_ref[z : z + 3].reshape(27 * channels, cells), preferred_element_type=F32
        )
        grads.append((grad_hidden * slope_ref[:, z * cells : (z + 1) * cells]).astype(BF16))
    grad_pre = jnp.concatenate(grads, axis=1)
    for a in range(3):
        out = jnp.dot(grad_pre, window(xf_ref, 1 + a, planes), preferred_element_type=F32)
        for rest in range(9):
            tap = a * 9 + rest
            total_ref[tap * channels : (tap + 1) * channels] = out[
                :, rest * channels : (rest + 1) * channels
            ].T
    split_terms(me, total_ref, send_ref, keep_ref)


def hidden_kernel(count, me_ref, xf_ref, bank_ref, hidden_ref, xh_ref):
    me = me_ref[0]
    planes, height, width, channels = hidden_ref.shape
    for at, first, inside in ((0, 0, me > 0), (planes + 1, planes + 1, me < count - 1)):
        active, _ = gelu_parts(conv_rows(xf_ref, first, 1, bank_ref))
        active = jnp.where(inside, active, 0.0)
        write_shifted(xh_ref, at, active.astype(BF16).reshape(height, width, channels))
    for p in range(planes):
        write_shifted(xh_ref, p + 1, hidden_ref[p])


def output_kernel(xh_ref, second_ref, out_ref):
    out = conv_rows(xh_ref, 0, out_ref.shape[0], second_ref)
    out_ref[...] = out.astype(BF16).reshape(out_ref.shape)


def scatter_bits(me):
    low = me % 2 == 0
    y, z = (me // 2) % 2, (me // 4) % 2
    return low, jnp.where(low, y, z), jnp.where(low, z, y), me // 8


def sum_pair_kernel(me_ref, *refs):
    keep_refs, got_refs, (far_send, send, far_own, own) = refs[:2], refs[2:4], refs[4:]
    low, first, _, last = scatter_bits(me_ref[0])
    for bank, (keep_ref, got_ref) in enumerate(zip(keep_refs, got_refs)):
        for second in range(2):
            at = 2 * bank + second
            for side, send_ref, own_ref in ((1 - last, far_send, far_own), (last, send, own)):

                def total(bit):
                    k = 4 * side + jnp.where(low, 2 * second + bit, 2 * bit + second)
                    return keep_ref[k] + got_ref[k].astype(F32)

                own_ref[at] = total(first)
                send_ref[at] = total(1 - first).astype(BF16)


def sum_near_kernel(me_ref, own_ref, got_ref, send_ref, keep_ref):
    _, _, second, _ = scatter_bits(me_ref[0])
    for bank in range(2):
        mine, other = 2 * bank + second, 2 * bank + 1 - second
        keep_ref[bank] = own_ref[mine] + got_ref[mine].astype(F32)
        send_ref[bank] = (own_ref[other] + got_ref[other].astype(F32)).astype(BF16)


def sum_far_kernel(keep_ref, got_ref, send_ref):
    send_ref[...] = (keep_ref[...] + got_ref[...].astype(F32)).astype(BF16)


def sum_last_kernel(keep_ref, near_ref, far_ref, first_ref, second_ref):
    for bank, ref in enumerate((first_ref, second_ref)):
        ref[...] = keep_ref[bank] + near_ref[bank].astype(F32) + far_ref[bank].astype(F32)


def swap(value, count, distance):
    return lax.ppermute(value, "slab", [(i, i ^ distance) for i in range(count)])


def swap_mixed(value, count, even, odd):
    pairs = [(i, i ^ (odd if i % 2 else even)) for i in range(count)]
    return lax.ppermute(value, "slab", pairs)


def joined(parts, name, wait_for=()):
    depth = sum(part.shape[0] if part.ndim == 3 else 1 for part in parts)
    out = like((depth, *parts[0].shape[-2:]), BF16)
    return local_call(join_kernel, name, [out], parts, wait_for=wait_for)[0]


def shards(count, features, filters_first, filters_second, cotangent):
    planes, height, width, channels = features.shape
    cells = planes * height * width
    rows = filters_first.shape[0]
    taps = 27 * channels
    direct = count == 16 and rows % 8 == 0
    me = lax.axis_index("slab").astype(jnp.int32).reshape(1)
    shard_rows = rows if direct else taps // 16
    place = me if direct else jnp.zeros((1,), jnp.int32)
    order = assemble if direct else assemble_in_order

    edge = like((3, height, width, channels), BF16)
    to_core, to_chip = from_hbm(edges_kernel, "edges", [edge, edge], [features, cotangent], [me])
    (own,) = from_hbm(
        load_shards_kernel,
        "load_shards",
        [like((2, rows, channels), BF16)],
        [filters_first, filters_second],
    )
    features, cotangent = from_hbm(
        load_kernel,
        "load",
        [like(features.shape, BF16), like(cotangent.shape, BF16)],
        [features, cotangent],
        wait_for=[to_chip],
    )
    from_core = swap(to_core, count, 1)
    next_chip = [(i, i + 1 if i % 2 else i - 1) for i in range(1, count - 1)]
    from_chip = lax.ppermute(to_chip, "slab", next_chip)
    xf, xg, gt = local_call(
        prepare_kernel,
        "shifted_planes",
        [
            like((planes + 4, height + 2, width, 3 * channels), BF16),
            like((planes + 2, height + 2, width, 3 * channels), BF16),
            like((planes + 2, 9, channels, height * width), BF16),
        ],
        [me, features, cotangent, from_core, from_chip],
        scalars=1,
    )
    wait_for = []
    if direct:
        far = swap(own, count, 8)
        near = swap_mixed(own, count, 4, 2)
        close = joined([own, near], "own_and_near", [])
        cross = swap_mixed(close, count, 2, 4)
        near = swap_mixed(far, count, 4, 2)
        away = joined([far, near], "far_and_near", [xf])
        cross_away = swap_mixed(away, count, 2, 4)
        pieces = [close, away, cross, cross_away]
        pieces += [swap(piece, count, 1) for piece in pieces]
    else:
        pieces = [
            lax.all_gather(shard, "slab", axis=0, tiled=True)
            for shard in (filters_first, filters_second)
        ]
    terms = [like((8, shard_rows, channels), BF16), like((8, shard_rows, channels), F32)]
    total = pltpu.VMEM((taps, channels), F32)
    bank, hidden, slope, send_second, keep_second = local_call(
        functools.partial(first_kernel, len(pieces), order),
        "hidden_and_second_grad",
        [
            like((taps, channels), BF16),
            like(features.shape, BF16),
            like((channels, cells), F32),
            *terms,
        ],
        [place, *pieces, xf, xg],
        scratch=[total],
        scalars=1,
        wait_for=wait_for,
    )
    bank_second, send_first, keep_first = local_call(
        functools.partial(second_kernel, len(pieces), order),
        "first_grad",
        [like((taps, channels), BF16), *terms],
        [place, *pieces, xf, gt, slope],
        scratch=[total],
        scalars=1,
    )
    wait_for = [keep_first]
    if direct:
        got_second = swap(send_second, count, 1)
        wait_for.append(got_second)
    (xh,) = local_call(
        functools.partial(hidden_kernel, count),
        "hidden_planes",
        [like((planes + 2, height + 2, width, 3 * channels), BF16)],
        [me, xf, bank, hidden],
        scalars=1,
        wait_for=wait_for,
    )
    wait_for = []
    if direct:
        blocks = [like((4, rows, channels), BF16)] * 2 + [like((4, rows, channels), F32)] * 2
        far_send, send, far_own, own = local_call(
            sum_pair_kernel,
            "sum_pair",
            blocks,
            [
                me,
                keep_first,
                keep_second,
                swap(send_first, count, 1),
                got_second,
            ],
            scalars=1,
            wait_for=[xh],
        )
        halves = [like((2, rows, channels), BF16), like((2, rows, channels), F32)]
        far_got = swap_mixed(far_send, count, 2, 4)
        far_send, far_keep = local_call(
            sum_near_kernel, "far_near", halves, [me, far_own, far_got], scalars=1
        )
        far_got = swap_mixed(far_send, count, 4, 2)
        got = swap_mixed(send, count, 2, 4)
        send, keep = local_call(
            sum_near_kernel, "own_near", halves, [me, own, got], scalars=1, wait_for=[far_send]
        )
        got = swap_mixed(send, count, 4, 2)
        (far_send,) = local_call(
            sum_far_kernel, "far_last", halves[:1], [far_keep, far_got]
        )
        far_got = swap(far_send, count, 8)
        wait_for = [far_send]
    (output,) = local_call(
        output_kernel, "output_conv", [like(features.shape, BF16)], [xh, bank_second], wait_for=wait_for
    )
    if direct:
        out = like((rows, channels), F32)
        grad_first, grad_second = local_call(
            sum_last_kernel, "sum_last", [out, out], [keep, got, far_got]
        )
    else:
        grad_first, grad_second = (
            lax.psum_scatter(
                jnp.stack([keep, send.astype(F32)], 1).reshape(taps, channels),
                "slab",
                scatter_dimension=0,
                tiled=True,
            )
            for send, keep in ((send_first, keep_first), (send_second, keep_second))
        )
    return (output, grad_first, grad_second)


def solution(mesh):
    return jax.shard_map(
        functools.partial(shards, mesh.shape["slab"]),
        mesh=mesh,
        in_specs=(
            P(("groups", "slab"), None, None, None),
            P("slab", None),
            P("slab", None),
            P(("groups", "slab"), None, None, None),
        ),
        out_specs=(
            P(("groups", "slab"), None, None, None),
            P(("groups", "slab"), None),
            P(("groups", "slab"), None),
        ),
        check_vma=False,
    )
```

```python
import functools

import jax
import jax.numpy as jnp
from jax import lax
from jax.experimental import pallas as pl
from jax.experimental.pallas import tpu as pltpu
from jax.sharding import PartitionSpec as P

inv_root_two = 0.7071067811865476
inv_root_two_pi = 0.3989422804014327

BF16 = jnp.bfloat16
F32 = jnp.float32
LIMIT = 14 << 20


def gelu_parts(value):
    normal_cdf = 0.5 * (1.0 + lax.erf(value * inv_root_two))
    slope = normal_cdf + value * jnp.exp(-0.5 * value * value) * inv_root_two_pi
    return (value * normal_cdf, slope)


def local_call(kernel, name, outs, args, scratch=(), scalars=0, wait_for=()):
    first, last = len(args), len(args) + len(wait_for)

    def body(*refs):
        kernel(*refs[:first], *refs[last:])

    spaces = [pltpu.SMEM] * scalars + [pltpu.VMEM] * (first - scalars) + [pl.ANY] * len(wait_for)
    return pl.pallas_call(
        body,
        out_shape=list(outs),
        in_specs=[pl.BlockSpec(memory_space=space) for space in spaces],
        out_specs=[pl.BlockSpec(memory_space=pltpu.VMEM) for _ in outs],
        scratch_shapes=list(scratch),
        name=name,
        compiler_params=pltpu.CompilerParams(vmem_limit_bytes=LIMIT),
        cost_estimate=pl.CostEstimate(flops=1000, bytes_accessed=0, transcendentals=0),
    )(*args, *wait_for)


def like(shape, dtype):
    return jax.ShapeDtypeStruct(shape, dtype)


def write_shifted(dst, at, plane):
    height, width, channels = plane.shape
    flat = plane.astype(F32).reshape(height * width, channels)
    column = lax.broadcasted_iota(jnp.int32, flat.shape, 0) % width
    left = jnp.where(column == 0, 0.0, pltpu.roll(flat, 1, 0))
    right = jnp.where(column == width - 1, 0.0, pltpu.roll(flat, height * width - 1, 0))
    row = jnp.zeros((1, width, 3 * channels), BF16)
    dst[at, 0:1] = row
    dst[at, height + 1 : height + 2] = row
    for block, value in enumerate((left, flat, right)):
        dst[at, 1 : height + 1, :, block * channels : (block + 1) * channels] = (
            value.astype(BF16).reshape(height, width, channels)
        )


def sides(me_ref, core_ref, chip_ref, own):
    odd = me_ref[0] % 2
    for ref, below in ((core_ref, odd == 1), (chip_ref, odd == 0)):
        yield ref, lambda p, count: jnp.where(below, p, own + count + p)


def features_kernel(me_ref, f_ref, core_ref, chip_ref, xf_ref):
    planes = f_ref.shape[0]
    for ref, place in sides(me_ref, core_ref, chip_ref, planes):
        for p in range(2):
            write_shifted(xf_ref, place(p, 2), ref[p])
    for p in range(planes):
        write_shifted(xf_ref, p + 2, f_ref[p])


def cotangent_kernel(me_ref, g_ref, core_ref, chip_ref, xg_ref, gt_ref):
    planes, height, width, channels = g_ref.shape
    for ref, place in sides(me_ref, core_ref, chip_ref, planes):
        write_shifted(xg_ref, place(0, 1), ref[2])
    for p in range(planes):
        write_shifted(xg_ref, p + 1, g_ref[p])

    def transposed(p, _):
        for b in range(3):
            for c in range(3):
                block = xg_ref[p, b : b + height, :, c * channels : (c + 1) * channels]
                gt_ref[p, b * 3 + c] = block.reshape(height * width, channels).T
        return 0

    lax.fori_loop(0, planes + 2, transposed, 0)


def copy_all(moves, sems):
    copies = [
        pltpu.make_async_copy(source, target, sems.at[at])
        for at, (source, target) in enumerate(moves)
    ]
    for copy in copies:
        copy.start()
    for copy in copies:
        copy.wait()


def load_kernel(f_hbm, g_hbm, f_ref, g_ref, sems):
    copy_all(((f_hbm, f_ref), (g_hbm, g_ref)), sems)


def first_load_kernel(me_ref, f_hbm, g_hbm, first_hbm, second_hbm, *refs):
    shards_ref, core_ref, chip_ref, sems = refs
    planes = f_hbm.shape[0]
    odd = me_ref[0] % 2
    moves = [(first_hbm, shards_ref.at[0]), (second_hbm, shards_ref.at[1])]
    for ref, low in ((chip_ref, odd == 0), (core_ref, odd == 1)):
        moves.append((f_hbm.at[pl.ds(jnp.where(low, 0, planes - 2), 2)], ref.at[pl.ds(0, 2)]))
        moves.append((g_hbm.at[pl.ds(jnp.where(low, 0, planes - 1), 1)], ref.at[pl.ds(2, 1)]))
    copy_all(moves, sems)


def from_hbm(kernel, name, outs, args, scalars=(), wait_for=()):
    args = [pltpu.with_memory_space_constraint(a, pltpu.HBM) for a in args]
    first, last = len(scalars) + len(args), len(scalars) + len(args) + len(wait_for)

    def body(*refs):
        kernel(*refs[:first], *refs[last:])

    spaces = [pltpu.SMEM] * len(scalars) + [pltpu.HBM] * len(args) + [pl.ANY] * len(wait_for)
    return pl.pallas_call(
        body,
        out_shape=outs,
        in_specs=[pl.BlockSpec(memory_space=space) for space in spaces],
        out_specs=[pl.BlockSpec(memory_space=pltpu.VMEM) for _ in outs],
        scratch_shapes=[pltpu.SemaphoreType.DMA((6,))],
        name=name,
        compiler_params=pltpu.CompilerParams(vmem_limit_bytes=LIMIT),
        cost_estimate=pl.CostEstimate(flops=1000, bytes_accessed=0, transcendentals=0),
    )(*scalars, *args, *wait_for)


def join_kernel(*refs):
    *parts, out_ref = refs
    at = 0
    for part in parts:
        if len(part.shape) == 2:
            out_ref[at] = part[...]
            at += 1
        else:
            out_ref[at : at + part.shape[0]] = part[...]
            at += part.shape[0]


def window(ref, first, planes):
    height, width, lanes = ref.shape[1] - 2, ref.shape[2], ref.shape[3]
    return jnp.concatenate(
        [
            ref[first : first + planes, b : b + height].reshape(planes * height * width, lanes)
            for b in range(3)
        ],
        axis=1,
    )


def conv_rows(ref, first, planes, weight_ref):
    depth = weight_ref.shape[0] // 3
    cells = (ref.shape[1] - 2) * ref.shape[2]
    taps = [weight_ref[a * depth : (a + 1) * depth] for a in range(3)]

    def term(at, count, weight):
        return jnp.dot(window(ref, first + at, count), weight, preferred_element_type=F32)

    if planes == 1:
        return sum(term(a, 1, taps[a]) for a in range(3))
    channels = taps[0].shape[1]
    middle = term(1, planes - 1, jnp.concatenate(taps[:2], axis=1))
    late = term(2, planes - 2, taps[2])
    ends = (term(0, 1, taps[0]), term(planes + 1, 1, taps[2]))
    last = term(planes, 1, jnp.concatenate(taps[1:], axis=1))
    parts = [[] for _ in range(planes)]
    parts[0].append(ends[0])
    for p in range(1, planes):
        rows = slice((p - 1) * cells, p * cells)
        parts[p].append(middle[rows, :channels])
        parts[p - 1].append(middle[rows, channels:])
    for p in range(2, planes):
        parts[p - 2].append(late[(p - 2) * cells : (p - 1) * cells])
    parts[planes - 1].append(last[:, :channels])
    parts[planes - 2].append(last[:, channels:])
    parts[planes - 1].append(ends[1])
    return jnp.concatenate([sum(terms[1:], terms[0]) for terms in parts], axis=0)


def near_far(core):
    return jnp.where(core == 0, 4, 2), jnp.where(core == 0, 2, 4)


def assemble(bank, me, pieces, dst):
    rows = pieces[0].shape[1]
    near, far = near_far(me % 2)
    starts = (me, me ^ 8, me ^ far, me ^ 8 ^ far)
    starts += tuple(start ^ 1 for start in (me, me ^ 8, me ^ near, me ^ 8 ^ near))
    for at, (piece, start) in enumerate(zip(pieces, starts)):
        for next_to, owner in enumerate((start, start ^ (near if at < 4 else far))):
            dst[pl.ds(pl.multiple_of(owner * rows, 8), rows)] = piece[2 * next_to + bank]


def assemble_in_order(bank, me, pieces, dst):
    dst[...] = pieces[bank][...]


def split_terms(me, total_ref, send_ref, keep_ref):
    count, rows, _ = keep_ref.shape
    core = me % 2
    for k in range(count):
        own = pl.multiple_of((2 * k + core) * rows, 8)
        other = pl.multiple_of((2 * k + 1 - core) * rows, 8)
        keep_ref[k] = total_ref[pl.ds(own, rows)]
        send_ref[k] = total_ref[pl.ds(other, rows)].astype(BF16)


def first_kernel(pieces, place, me_ref, *refs):
    piece_refs, (xf_ref, xg_ref, *out_refs) = refs[:pieces], refs[pieces:]
    bank_ref, hidden_ref, slope_ref, send_ref, keep_ref, total_ref = out_refs
    me = me_ref[0]
    planes, height, width, channels = hidden_ref.shape
    place(0, me, piece_refs, bank_ref)
    active, slope = gelu_parts(conv_rows(xf_ref, 1, planes, bank_ref))
    slope_ref[...] = slope.T
    hidden = active.astype(BF16)
    hidden_ref[...] = hidden.reshape(hidden_ref.shape)
    flipped = hidden.T
    for a in range(3):
        out = jnp.dot(flipped, window(xg_ref, 2 - a, planes), preferred_element_type=F32)
        for rest in range(9):
            tap, source = a * 9 + rest, 8 - rest
            total_ref[tap * channels : (tap + 1) * channels] = out[
                :, source * channels : (source + 1) * channels
            ]
    split_terms(me, total_ref, send_ref, keep_ref)


def second_kernel(pieces, place, me_ref, *refs):
    piece_refs, (xf_ref, gt_ref, slope_ref, *out_refs) = refs[:pieces], refs[pieces:]
    bank_ref, send_ref, keep_ref, total_ref = out_refs
    me = me_ref[0]
    channels = slope_ref.shape[0]
    planes, _, _, cells = gt_ref.shape
    planes -= 2
    place(1, me, piece_refs, bank_ref)
    back = jnp.concatenate(
        [bank_ref[tap * channels : (tap + 1) * channels] for tap in reversed(range(27))], axis=1
    )
    grads = []
    for z in range(planes):
        grad_hidden = jnp.dot(
            back, gt_ref[z : z + 3].reshape(27 * channels, cells), preferred_element_type=F32
        )
        grads.append((grad_hidden * slope_ref[:, z * cells : (z + 1) * cells]).astype(BF16))
    grad_pre = jnp.concatenate(grads, axis=1)
    for a in range(3):
        out = jnp.dot(grad_pre, window(xf_ref, 1 + a, planes), preferred_element_type=F32)
        for rest in range(9):
            tap = a * 9 + rest
            total_ref[tap * channels : (tap + 1) * channels] = out[
                :, rest * channels : (rest + 1) * channels
            ].T
    split_terms(me, total_ref, send_ref, keep_ref)


def hidden_kernel(count, me_ref, xf_ref, bank_ref, hidden_ref, xh_ref):
    me = me_ref[0]
    planes, height, width, channels = hidden_ref.shape
    for at, first, inside in ((0, 0, me > 0), (planes + 1, planes + 1, me < count - 1)):
        active, _ = gelu_parts(conv_rows(xf_ref, first, 1, bank_ref))
        active = jnp.where(inside, active, 0.0)
        write_shifted(xh_ref, at, active.astype(BF16).reshape(height, width, channels))
    for p in range(planes):
        write_shifted(xh_ref, p + 1, hidden_ref[p])


def output_kernel(xh_ref, second_ref, out_ref):
    out = conv_rows(xh_ref, 0, out_ref.shape[0], second_ref)
    out_ref[...] = out.astype(BF16).reshape(out_ref.shape)


def scatter_bits(me):
    low = me % 2 == 0
    y, z = (me // 2) % 2, (me // 4) % 2
    return low, jnp.where(low, y, z), jnp.where(low, z, y), me // 8


def sum_pair_kernel(me_ref, *refs):
    keep_refs, got_refs, (far_send, send, far_own, own) = refs[:2], refs[2:4], refs[4:]
    low, first, _, last = scatter_bits(me_ref[0])
    for bank, (keep_ref, got_ref) in enumerate(zip(keep_refs, got_refs)):
        for second in range(2):
            at = 2 * bank + second
            for side, send_ref, own_ref in ((1 - last, far_send, far_own), (last, send, own)):

                def total(bit):
                    k = 4 * side + jnp.where(low, 2 * second + bit, 2 * bit + second)
                    return keep_ref[k] + got_ref[k].astype(F32)

                own_ref[at] = total(first)
                send_ref[at] = total(1 - first).astype(BF16)


def sum_near_kernel(me_ref, own_ref, got_ref, send_ref, keep_ref):
    _, _, second, _ = scatter_bits(me_ref[0])
    for bank in range(2):
        mine, other = 2 * bank + second, 2 * bank + 1 - second
        keep_ref[bank] = own_ref[mine] + got_ref[mine].astype(F32)
        send_ref[bank] = (own_ref[other] + got_ref[other].astype(F32)).astype(BF16)


def sum_far_kernel(keep_ref, got_ref, send_ref):
    send_ref[...] = (keep_ref[...] + got_ref[...].astype(F32)).astype(BF16)


def sum_last_kernel(keep_ref, near_ref, far_ref, first_ref, second_ref):
    for bank, ref in enumerate((first_ref, second_ref)):
        ref[...] = keep_ref[bank] + near_ref[bank].astype(F32) + far_ref[bank].astype(F32)


def swap(value, count, distance):
    return lax.ppermute(value, "slab", [(i, i ^ distance) for i in range(count)])


def swap_mixed(value, count, even, odd):
    pairs = [(i, i ^ (odd if i % 2 else even)) for i in range(count)]
    return lax.ppermute(value, "slab", pairs)


def joined(parts, name, wait_for=()):
    depth = sum(part.shape[0] if part.ndim == 3 else 1 for part in parts)
    out = like((depth, *parts[0].shape[-2:]), BF16)
    return local_call(join_kernel, name, [out], parts, wait_for=wait_for)[0]


def shards(count, features, filters_first, filters_second, cotangent):
    planes, height, width, channels = features.shape
    cells = planes * height * width
    rows = filters_first.shape[0]
    taps = 27 * channels
    direct = count == 16 and rows % 8 == 0
    me = lax.axis_index("slab").astype(jnp.int32).reshape(1)
    shard_rows = rows if direct else taps // 16
    place = me if direct else jnp.zeros((1,), jnp.int32)
    order = assemble if direct else assemble_in_order

    edge = like((3, height, width, channels), BF16)
    own, to_core, to_chip = from_hbm(
        first_load_kernel,
        "load_shards_and_edges",
        [like((2, rows, channels), BF16), edge, edge],
        [features, cotangent, filters_first, filters_second],
        [me],
    )
    features, cotangent = from_hbm(
        load_kernel,
        "load",
        [like(features.shape, BF16), like(cotangent.shape, BF16)],
        [features, cotangent],
        wait_for=[to_chip],
    )
    from_core = swap(to_core, count, 1)
    next_chip = [(i, i + 1 if i % 2 else i - 1) for i in range(1, count - 1)]
    from_chip = lax.ppermute(to_chip, "slab", next_chip)
    edges = [from_core, from_chip]
    (xf,) = local_call(
        features_kernel,
        "feature_planes",
        [like((planes + 4, height + 2, width, 3 * channels), BF16)],
        [me, features, *edges],
        scalars=1,
    )
    wait_for = []
    if direct:
        far = swap(own, count, 8)
        near = swap_mixed(own, count, 4, 2)
        close = joined([own, near], "own_and_near", [])
        cross = swap_mixed(close, count, 2, 4)
        near = swap_mixed(far, count, 4, 2)
        away = joined([far, near], "far_and_near", [xf])
        cross_away = swap_mixed(away, count, 2, 4)
        wait_for = [cross_away]
        pieces = [close, away, cross, cross_away]
        pieces += [swap(piece, count, 1) for piece in pieces]
    else:
        pieces = [
            lax.all_gather(shard, "slab", axis=0, tiled=True)
            for shard in (filters_first, filters_second)
        ]
    xg, gt = local_call(
        cotangent_kernel,
        "cotangent_planes",
        [
            like((planes + 2, height + 2, width, 3 * channels), BF16),
            like((planes + 2, 9, channels, height * width), BF16),
        ],
        [me, cotangent, *edges],
        scalars=1,
        wait_for=wait_for,
    )
    terms = [like((8, shard_rows, channels), BF16), like((8, shard_rows, channels), F32)]
    total = pltpu.VMEM((taps, channels), F32)
    bank, hidden, slope, send_second, keep_second = local_call(
        functools.partial(first_kernel, len(pieces), order),
        "hidden_and_second_grad",
        [
            like((taps, channels), BF16),
            like(features.shape, BF16),
            like((channels, cells), F32),
            *terms,
        ],
        [place, *pieces, xf, xg],
        scratch=[total],
        scalars=1,
    )
    bank_second, send_first, keep_first = local_call(
        functools.partial(second_kernel, len(pieces), order),
        "first_grad",
        [like((taps, channels), BF16), *terms],
        [place, *pieces, xf, gt, slope],
        scratch=[total],
        scalars=1,
    )
    wait_for = [keep_first]
    if direct:
        got_second = swap(send_second, count, 1)
        wait_for.append(got_second)
    (xh,) = local_call(
        functools.partial(hidden_kernel, count),
        "hidden_planes",
        [like((planes + 2, height + 2, width, 3 * channels), BF16)],
        [me, xf, bank, hidden],
        scalars=1,
        wait_for=wait_for,
    )
    wait_for = []
    if direct:
        blocks = [like((4, rows, channels), BF16)] * 2 + [like((4, rows, channels), F32)] * 2
        far_send, send, far_own, own = local_call(
            sum_pair_kernel,
            "sum_pair",
            blocks,
            [
                me,
                keep_first,
                keep_second,
                swap(send_first, count, 1),
                got_second,
            ],
            scalars=1,
            wait_for=[xh],
        )
        halves = [like((2, rows, channels), BF16), like((2, rows, channels), F32)]
        far_got = swap_mixed(far_send, count, 2, 4)
        far_send, far_keep = local_call(
            sum_near_kernel, "far_near", halves, [me, far_own, far_got], scalars=1
        )
        far_got = swap_mixed(far_send, count, 4, 2)
        got = swap_mixed(send, count, 2, 4)
        send, keep = local_call(
            sum_near_kernel, "own_near", halves, [me, own, got], scalars=1, wait_for=[far_send]
        )
        got = swap_mixed(send, count, 4, 2)
        (far_send,) = local_call(
            sum_far_kernel, "far_last", halves[:1], [far_keep, far_got]
        )
        far_got = swap(far_send, count, 8)
        wait_for = [far_send]
    (output,) = local_call(
        output_kernel, "output_conv", [like(features.shape, BF16)], [xh, bank_second], wait_for=wait_for
    )
    if direct:
        out = like((rows, channels), F32)
        grad_first, grad_second = local_call(
            sum_last_kernel, "sum_last", [out, out], [keep, got, far_got]
        )
    else:
        grad_first, grad_second = (
            lax.psum_scatter(
                jnp.stack([keep, send.astype(F32)], 1).reshape(taps, channels),
                "slab",
                scatter_dimension=0,
                tiled=True,
            )
            for send, keep in ((send_first, keep_first), (send_second, keep_second))
        )
    return (output, grad_first, grad_second)


def solution(mesh):
    return jax.shard_map(
        functools.partial(shards, mesh.shape["slab"]),
        mesh=mesh,
        in_specs=(
            P(("groups", "slab"), None, None, None),
            P("slab", None),
            P("slab", None),
            P(("groups", "slab"), None, None, None),
        ),
        out_specs=(
            P(("groups", "slab"), None, None, None),
            P(("groups", "slab"), None),
            P(("groups", "slab"), None),
        ),
        check_vma=False,
    )
```

```python
import functools

import jax
import jax.numpy as jnp
from jax import lax
from jax.experimental import pallas as pl
from jax.experimental.pallas import tpu as pltpu
from jax.sharding import PartitionSpec as P

inv_root_two = 0.7071067811865476
inv_root_two_pi = 0.3989422804014327

BF16 = jnp.bfloat16
F32 = jnp.float32
LIMIT = 14 << 20


def gelu_parts(value):
    normal_cdf = 0.5 * (1.0 + lax.erf(value * inv_root_two))
    slope = normal_cdf + value * jnp.exp(-0.5 * value * value) * inv_root_two_pi
    return (value * normal_cdf, slope)


def local_call(kernel, name, outs, args, scratch=(), scalars=0, wait_for=()):
    first, last = len(args), len(args) + len(wait_for)

    def body(*refs):
        kernel(*refs[:first], *refs[last:])

    spaces = [pltpu.SMEM] * scalars + [pltpu.VMEM] * (first - scalars) + [pl.ANY] * len(wait_for)
    return pl.pallas_call(
        body,
        out_shape=list(outs),
        in_specs=[pl.BlockSpec(memory_space=space) for space in spaces],
        out_specs=[pl.BlockSpec(memory_space=pltpu.VMEM) for _ in outs],
        scratch_shapes=list(scratch),
        name=name,
        compiler_params=pltpu.CompilerParams(vmem_limit_bytes=LIMIT),
        cost_estimate=pl.CostEstimate(flops=1000, bytes_accessed=0, transcendentals=0),
    )(*args, *wait_for)


def like(shape, dtype):
    return jax.ShapeDtypeStruct(shape, dtype)


def write_shifted(dst, at, plane):
    height, width, channels = plane.shape
    flat = plane.astype(F32).reshape(height * width, channels)
    column = lax.broadcasted_iota(jnp.int32, flat.shape, 0) % width
    left = jnp.where(column == 0, 0.0, pltpu.roll(flat, 1, 0))
    right = jnp.where(column == width - 1, 0.0, pltpu.roll(flat, height * width - 1, 0))
    row = jnp.zeros((1, width, 3 * channels), BF16)
    dst[at, 0:1] = row
    dst[at, height + 1 : height + 2] = row
    for block, value in enumerate((left, flat, right)):
        dst[at, 1 : height + 1, :, block * channels : (block + 1) * channels] = (
            value.astype(BF16).reshape(height, width, channels)
        )


def sides(me_ref, core_ref, chip_ref, own):
    odd = me_ref[0] % 2
    for ref, below in ((core_ref, odd == 1), (chip_ref, odd == 0)):
        yield ref, lambda p, count: jnp.where(below, p, own + count + p)


def features_kernel(me_ref, f_ref, core_ref, chip_ref, xf_ref):
    planes = f_ref.shape[0]
    for ref, place in sides(me_ref, core_ref, chip_ref, planes):
        for p in range(2):
            write_shifted(xf_ref, place(p, 2), ref[p])
    for p in range(planes):
        write_shifted(xf_ref, p + 2, f_ref[p])


def cotangent_kernel(me_ref, g_ref, core_ref, chip_ref, xg_ref, gt_ref):
    planes, height, width, channels = g_ref.shape
    for ref, place in sides(me_ref, core_ref, chip_ref, planes):
        write_shifted(xg_ref, place(0, 1), ref[2])
    for p in range(planes):
        write_shifted(xg_ref, p + 1, g_ref[p])

    def transposed(p, _):
        for b in range(3):
            for c in range(3):
                block = xg_ref[p, b : b + height, :, c * channels : (c + 1) * channels]
                gt_ref[p, b * 3 + c] = block.reshape(height * width, channels).T
        return 0

    lax.fori_loop(0, planes + 2, transposed, 0)


def copy_all(moves, sems):
    copies = [
        pltpu.make_async_copy(source, target, sems.at[at])
        for at, (source, target) in enumerate(moves)
    ]
    for copy in copies:
        copy.start()
    for copy in copies:
        copy.wait()


def load_kernel(f_hbm, g_hbm, f_ref, g_ref, sems):
    copy_all(((f_hbm, f_ref), (g_hbm, g_ref)), sems)


def first_load_kernel(me_ref, f_hbm, g_hbm, first_hbm, second_hbm, *refs):
    shards_ref, core_ref, chip_ref, sems = refs
    planes = f_hbm.shape[0]
    odd = me_ref[0] % 2
    moves = [(first_hbm, shards_ref.at[0]), (second_hbm, shards_ref.at[1])]
    for ref, low in ((chip_ref, odd == 0), (core_ref, odd == 1)):
        moves.append((f_hbm.at[pl.ds(jnp.where(low, 0, planes - 2), 2)], ref.at[pl.ds(0, 2)]))
        moves.append((g_hbm.at[pl.ds(jnp.where(low, 0, planes - 1), 1)], ref.at[pl.ds(2, 1)]))
    copy_all(moves, sems)


def from_hbm(kernel, name, outs, args, scalars=(), wait_for=()):
    args = [pltpu.with_memory_space_constraint(a, pltpu.HBM) for a in args]
    first, last = len(scalars) + len(args), len(scalars) + len(args) + len(wait_for)

    def body(*refs):
        kernel(*refs[:first], *refs[last:])

    spaces = [pltpu.SMEM] * len(scalars) + [pltpu.HBM] * len(args) + [pl.ANY] * len(wait_for)
    return pl.pallas_call(
        body,
        out_shape=outs,
        in_specs=[pl.BlockSpec(memory_space=space) for space in spaces],
        out_specs=[pl.BlockSpec(memory_space=pltpu.VMEM) for _ in outs],
        scratch_shapes=[pltpu.SemaphoreType.DMA((6,))],
        name=name,
        compiler_params=pltpu.CompilerParams(vmem_limit_bytes=LIMIT),
        cost_estimate=pl.CostEstimate(flops=1000, bytes_accessed=0, transcendentals=0),
    )(*scalars, *args, *wait_for)


def join_kernel(*refs):
    *parts, out_ref = refs
    at = 0
    for part in parts:
        if len(part.shape) == 2:
            out_ref[at] = part[...]
            at += 1
        else:
            out_ref[at : at + part.shape[0]] = part[...]
            at += part.shape[0]


def window(ref, first, planes):
    height, width, lanes = ref.shape[1] - 2, ref.shape[2], ref.shape[3]
    return jnp.concatenate(
        [
            ref[first : first + planes, b : b + height].reshape(planes * height * width, lanes)
            for b in range(3)
        ],
        axis=1,
    )


def conv_rows(ref, first, planes, weight_ref):
    depth = weight_ref.shape[0] // 3
    cells = (ref.shape[1] - 2) * ref.shape[2]
    taps = [weight_ref[a * depth : (a + 1) * depth] for a in range(3)]

    def term(at, count, weight):
        return jnp.dot(window(ref, first + at, count), weight, preferred_element_type=F32)

    if planes == 1:
        return sum(term(a, 1, taps[a]) for a in range(3))
    channels = taps[0].shape[1]
    middle = term(1, planes - 1, jnp.concatenate(taps[:2], axis=1))
    late = term(2, planes - 2, taps[2])
    ends = (term(0, 1, taps[0]), term(planes + 1, 1, taps[2]))
    last = term(planes, 1, jnp.concatenate(taps[1:], axis=1))
    parts = [[] for _ in range(planes)]
    parts[0].append(ends[0])
    for p in range(1, planes):
        rows = slice((p - 1) * cells, p * cells)
        parts[p].append(middle[rows, :channels])
        parts[p - 1].append(middle[rows, channels:])
    for p in range(2, planes):
        parts[p - 2].append(late[(p - 2) * cells : (p - 1) * cells])
    parts[planes - 1].append(last[:, :channels])
    parts[planes - 2].append(last[:, channels:])
    parts[planes - 1].append(ends[1])
    return jnp.concatenate([sum(terms[1:], terms[0]) for terms in parts], axis=0)


def near_far(core):
    return jnp.where(core == 0, 4, 2), jnp.where(core == 0, 2, 4)


def assemble(bank, me, pieces, dst):
    rows = pieces[0].shape[1]
    near, far = near_far(me % 2)
    starts = (me, me ^ 8, me ^ far, me ^ 8 ^ far)
    starts += tuple(start ^ 1 for start in (me, me ^ 8, me ^ near, me ^ 8 ^ near))
    for at, (piece, start) in enumerate(zip(pieces, starts)):
        for next_to, owner in enumerate((start, start ^ (near if at < 4 else far))):
            dst[pl.ds(pl.multiple_of(owner * rows, 8), rows)] = piece[2 * next_to + bank]


def assemble_in_order(bank, me, pieces, dst):
    dst[...] = pieces[bank][...]


def split_terms(me, total_ref, send_ref, keep_ref):
    count, rows, _ = keep_ref.shape
    core = me % 2
    for k in range(count):
        own = pl.multiple_of((2 * k + core) * rows, 8)
        other = pl.multiple_of((2 * k + 1 - core) * rows, 8)
        keep_ref[k] = total_ref[pl.ds(own, rows)]
        send_ref[k] = total_ref[pl.ds(other, rows)].astype(BF16)


def first_kernel(pieces, place, me_ref, *refs):
    piece_refs, (xf_ref, xg_ref, *out_refs) = refs[:pieces], refs[pieces:]
    bank_ref, hidden_ref, slope_ref, send_ref, keep_ref, total_ref = out_refs
    me = me_ref[0]
    planes, height, width, channels = hidden_ref.shape
    place(0, me, piece_refs, bank_ref)
    active, slope = gelu_parts(conv_rows(xf_ref, 1, planes, bank_ref))
    slope_ref[...] = slope.T
    hidden = active.astype(BF16)
    hidden_ref[...] = hidden.reshape(hidden_ref.shape)
    flipped = hidden.T
    for a in range(3):
        out = jnp.dot(flipped, window(xg_ref, 2 - a, planes), preferred_element_type=F32)
        for rest in range(9):
            tap, source = a * 9 + rest, 8 - rest
            total_ref[tap * channels : (tap + 1) * channels] = out[
                :, source * channels : (source + 1) * channels
            ]
    split_terms(me, total_ref, send_ref, keep_ref)


def second_kernel(pieces, place, me_ref, *refs):
    piece_refs, (xf_ref, gt_ref, slope_ref, *out_refs) = refs[:pieces], refs[pieces:]
    bank_ref, send_ref, keep_ref, total_ref = out_refs
    me = me_ref[0]
    channels = slope_ref.shape[0]
    planes, _, _, cells = gt_ref.shape
    planes -= 2
    place(1, me, piece_refs, bank_ref)
    back = jnp.concatenate(
        [bank_ref[tap * channels : (tap + 1) * channels] for tap in reversed(range(27))], axis=1
    )
    grads = []
    for z in range(planes):
        grad_hidden = jnp.dot(
            back, gt_ref[z : z + 3].reshape(27 * channels, cells), preferred_element_type=F32
        )
        grads.append((grad_hidden * slope_ref[:, z * cells : (z + 1) * cells]).astype(BF16))
    grad_pre = jnp.concatenate(grads, axis=1)
    for a in range(3):
        out = jnp.dot(grad_pre, window(xf_ref, 1 + a, planes), preferred_element_type=F32)
        for rest in range(9):
            tap = a * 9 + rest
            total_ref[tap * channels : (tap + 1) * channels] = out[
                :, rest * channels : (rest + 1) * channels
            ].T
    split_terms(me, total_ref, send_ref, keep_ref)


def hidden_kernel(count, me_ref, xf_ref, bank_ref, hidden_ref, xh_ref):
    me = me_ref[0]
    planes, height, width, channels = hidden_ref.shape
    for at, first, inside in ((0, 0, me > 0), (planes + 1, planes + 1, me < count - 1)):
        active, _ = gelu_parts(conv_rows(xf_ref, first, 1, bank_ref))
        active = jnp.where(inside, active, 0.0)
        write_shifted(xh_ref, at, active.astype(BF16).reshape(height, width, channels))
    for p in range(planes):
        write_shifted(xh_ref, p + 1, hidden_ref[p])


def output_kernel(xh_ref, second_ref, out_ref):
    out = conv_rows(xh_ref, 0, out_ref.shape[0], second_ref)
    out_ref[...] = out.astype(BF16).reshape(out_ref.shape)


def scatter_bits(me):
    low = me % 2 == 0
    y, z = (me // 2) % 2, (me // 4) % 2
    return low, jnp.where(low, y, z), jnp.where(low, z, y), me // 8


def sum_pair_kernel(me_ref, keep_ref, got_ref, *refs):
    before, (far_send, far_own, send, own) = refs[:-4], refs[-4:]
    low, first, _, last = scatter_bits(me_ref[0])
    if before:
        for ref, earlier in zip((send, own), before):
            ref[2:4] = earlier[...]
    for second in range(2):
        for side, send_ref, own_ref in ((1 - last, far_send, far_own), (last, send, own)):

            def total(bit):
                k = 4 * side + jnp.where(low, 2 * second + bit, 2 * bit + second)
                return keep_ref[k] + got_ref[k].astype(F32)

            own_ref[second] = total(first)
            send_ref[second] = total(1 - first).astype(BF16)


def sum_near_kernel(me_ref, own_ref, got_ref, *refs):
    before, (send_ref, keep_ref) = refs[:-2], refs[-2:]
    _, _, second, _ = scatter_bits(me_ref[0])
    for bank in range(own_ref.shape[0] // 2):
        mine, other = 2 * bank + second, 2 * bank + 1 - second
        keep_ref[bank] = own_ref[mine] + got_ref[mine].astype(F32)
        send_ref[bank] = (own_ref[other] + got_ref[other].astype(F32)).astype(BF16)
    for ref, earlier in zip((send_ref, keep_ref), before):
        ref[1:2] = earlier[...]


def sum_far_kernel(keep_ref, got_ref, send_ref):
    send_ref[...] = (keep_ref[...] + got_ref[...].astype(F32)).astype(BF16)


def sum_last_kernel(keep_ref, near_ref, far_ref, first_ref, second_ref):
    for bank, ref in enumerate((first_ref, second_ref)):
        ref[...] = keep_ref[bank] + near_ref[bank].astype(F32) + far_ref[bank].astype(F32)


def swap(value, count, distance):
    return lax.ppermute(value, "slab", [(i, i ^ distance) for i in range(count)])


def swap_mixed(value, count, even, odd):
    pairs = [(i, i ^ (odd if i % 2 else even)) for i in range(count)]
    return lax.ppermute(value, "slab", pairs)


def joined(parts, name, wait_for=()):
    depth = sum(part.shape[0] if part.ndim == 3 else 1 for part in parts)
    out = like((depth, *parts[0].shape[-2:]), BF16)
    return local_call(join_kernel, name, [out], parts, wait_for=wait_for)[0]


def shards(count, features, filters_first, filters_second, cotangent):
    planes, height, width, channels = features.shape
    cells = planes * height * width
    rows = filters_first.shape[0]
    taps = 27 * channels
    direct = count == 16 and rows % 8 == 0
    me = lax.axis_index("slab").astype(jnp.int32).reshape(1)
    shard_rows = rows if direct else taps // 16
    place = me if direct else jnp.zeros((1,), jnp.int32)
    order = assemble if direct else assemble_in_order

    edge = like((3, height, width, channels), BF16)
    own, to_core, to_chip = from_hbm(
        first_load_kernel,
        "load_shards_and_edges",
        [like((2, rows, channels), BF16), edge, edge],
        [features, cotangent, filters_first, filters_second],
        [me],
    )
    features, cotangent = from_hbm(
        load_kernel,
        "load",
        [like(features.shape, BF16), like(cotangent.shape, BF16)],
        [features, cotangent],
        wait_for=[to_chip],
    )
    from_core = swap(to_core, count, 1)
    next_chip = [(i, i + 1 if i % 2 else i - 1) for i in range(1, count - 1)]
    from_chip = lax.ppermute(to_chip, "slab", next_chip)
    edges = [from_core, from_chip]
    (xf,) = local_call(
        features_kernel,
        "feature_planes",
        [like((planes + 4, height + 2, width, 3 * channels), BF16)],
        [me, features, *edges],
        scalars=1,
    )
    wait_for = []
    if direct:
        far = swap(own, count, 8)
        near = swap_mixed(own, count, 4, 2)
        close = joined([own, near], "own_and_near", [])
        cross = swap_mixed(close, count, 2, 4)
        near = swap_mixed(far, count, 4, 2)
        away = joined([far, near], "far_and_near", [xf])
        cross_away = swap_mixed(away, count, 2, 4)
        wait_for = [cross_away]
        pieces = [close, away, cross, cross_away]
        pieces += [swap(piece, count, 1) for piece in pieces]
    else:
        pieces = [
            lax.all_gather(shard, "slab", axis=0, tiled=True)
            for shard in (filters_first, filters_second)
        ]
    xg, gt = local_call(
        cotangent_kernel,
        "cotangent_planes",
        [
            like((planes + 2, height + 2, width, 3 * channels), BF16),
            like((planes + 2, 9, channels, height * width), BF16),
        ],
        [me, cotangent, *edges],
        scalars=1,
        wait_for=wait_for,
    )
    terms = [like((8, shard_rows, channels), BF16), like((8, shard_rows, channels), F32)]
    total = pltpu.VMEM((taps, channels), F32)
    bank, hidden, slope, send_second, keep_second = local_call(
        functools.partial(first_kernel, len(pieces), order),
        "hidden_and_second_grad",
        [
            like((taps, channels), BF16),
            like(features.shape, BF16),
            like((channels, cells), F32),
            *terms,
        ],
        [place, *pieces, xf, xg],
        scratch=[total],
        scalars=1,
    )
    bank_second, send_first, keep_first = local_call(
        functools.partial(second_kernel, len(pieces), order),
        "first_grad",
        [like((taps, channels), BF16), *terms],
        [place, *pieces, xf, gt, slope],
        scratch=[total],
        scalars=1,
    )
    def both(count):
        return [like((count, rows, channels), BF16), like((count, rows, channels), F32)]

    wait_for = [keep_first]
    if direct:
        far_send, far_own_second, *own_second = local_call(
            sum_pair_kernel,
            "second_pair",
            both(2) + both(2),
            [me, keep_second, swap(send_second, count, 1)],
            scalars=1,
        )
        far_got_second = swap_mixed(far_send, count, 2, 4)
        wait_for.append(far_send)
    (xh,) = local_call(
        functools.partial(hidden_kernel, count),
        "hidden_planes",
        [like((planes + 2, height + 2, width, 3 * channels), BF16)],
        [me, xf, bank, hidden],
        scalars=1,
        wait_for=wait_for,
    )
    wait_for = []
    if direct:
        far_send, far_own, send, own = local_call(
            sum_pair_kernel,
            "first_pair",
            both(2) + both(4),
            [me, keep_first, swap(send_first, count, 1), *own_second],
            scalars=1,
            wait_for=[xh],
        )
        far_got = swap_mixed(far_send, count, 2, 4)
        far_second = local_call(
            sum_near_kernel,
            "second_far_near",
            both(1),
            [me, far_own_second, far_got_second],
            scalars=1,
            wait_for=[far_send],
        )
        far_send, far_keep = local_call(
            sum_near_kernel, "first_far_near", both(2), [me, far_own, far_got, *far_second], scalars=1
        )
        far_got = swap_mixed(far_send, count, 4, 2)
        got = swap_mixed(send, count, 2, 4)
        send, keep = local_call(
            sum_near_kernel, "own_near", both(2), [me, own, got], scalars=1, wait_for=[far_send]
        )
        got = swap_mixed(send, count, 4, 2)
        (far_send,) = local_call(
            sum_far_kernel, "far_last", both(2)[:1], [far_keep, far_got]
        )
        far_got = swap(far_send, count, 8)
        wait_for = [far_send]
    (output,) = local_call(
        output_kernel, "output_conv", [like(features.shape, BF16)], [xh, bank_second], wait_for=wait_for
    )
    if direct:
        out = like((rows, channels), F32)
        grad_first, grad_second = local_call(
            sum_last_kernel, "sum_last", [out, out], [keep, got, far_got]
        )
    else:
        grad_first, grad_second = (
            lax.psum_scatter(
                jnp.stack([keep, send.astype(F32)], 1).reshape(taps, channels),
                "slab",
                scatter_dimension=0,
                tiled=True,
            )
            for send, keep in ((send_first, keep_first), (send_second, keep_second))
        )
    return (output, grad_first, grad_second)


def solution(mesh):
    return jax.shard_map(
        functools.partial(shards, mesh.shape["slab"]),
        mesh=mesh,
        in_specs=(
            P(("groups", "slab"), None, None, None),
            P("slab", None),
            P("slab", None),
            P(("groups", "slab"), None, None, None),
        ),
        out_specs=(
            P(("groups", "slab"), None, None, None),
            P(("groups", "slab"), None),
            P(("groups", "slab"), None),
        ),
        check_vma=False,
    )
```

```python
import functools

import jax
import jax.numpy as jnp
from jax import lax
from jax.experimental import pallas as pl
from jax.experimental.pallas import tpu as pltpu
from jax.sharding import PartitionSpec as P

inv_root_two = 0.7071067811865476
inv_root_two_pi = 0.3989422804014327

BF16 = jnp.bfloat16
F32 = jnp.float32
LIMIT = 14 << 20


def gelu_parts(value):
    normal_cdf = 0.5 * (1.0 + lax.erf(value * inv_root_two))
    slope = normal_cdf + value * jnp.exp(-0.5 * value * value) * inv_root_two_pi
    return (value * normal_cdf, slope)


def local_call(kernel, name, outs, args, scratch=(), scalars=0, wait_for=()):
    first, last = len(args), len(args) + len(wait_for)

    def body(*refs):
        kernel(*refs[:first], *refs[last:])

    spaces = [pltpu.SMEM] * scalars + [pltpu.VMEM] * (first - scalars) + [pl.ANY] * len(wait_for)
    return pl.pallas_call(
        body,
        out_shape=list(outs),
        in_specs=[pl.BlockSpec(memory_space=space) for space in spaces],
        out_specs=[pl.BlockSpec(memory_space=pltpu.VMEM) for _ in outs],
        scratch_shapes=list(scratch),
        name=name,
        compiler_params=pltpu.CompilerParams(vmem_limit_bytes=LIMIT),
        cost_estimate=pl.CostEstimate(flops=1000, bytes_accessed=0, transcendentals=0),
    )(*args, *wait_for)


def like(shape, dtype):
    return jax.ShapeDtypeStruct(shape, dtype)


def write_shifted(dst, at, plane):
    height, width, channels = plane.shape
    flat = plane.astype(F32).reshape(height * width, channels)
    column = lax.broadcasted_iota(jnp.int32, flat.shape, 0) % width
    left = jnp.where(column == 0, 0.0, pltpu.roll(flat, 1, 0))
    right = jnp.where(column == width - 1, 0.0, pltpu.roll(flat, height * width - 1, 0))
    row = jnp.zeros((1, width, 3 * channels), BF16)
    dst[at, 0:1] = row
    dst[at, height + 1 : height + 2] = row
    for block, value in enumerate((left, flat, right)):
        dst[at, 1 : height + 1, :, block * channels : (block + 1) * channels] = (
            value.astype(BF16).reshape(height, width, channels)
        )


def sides(me_ref, core_ref, chip_ref, own):
    odd = me_ref[0] % 2
    for ref, below in ((core_ref, odd == 1), (chip_ref, odd == 0)):
        yield ref, lambda p, count: jnp.where(below, p, own + count + p)


def features_kernel(me_ref, f_ref, core_ref, chip_ref, xf_ref):
    planes = f_ref.shape[0]
    for ref, place in sides(me_ref, core_ref, chip_ref, planes):
        for p in range(2):
            write_shifted(xf_ref, place(p, 2), ref[p])
    for p in range(planes):
        write_shifted(xf_ref, p + 2, f_ref[p])


def cotangent_kernel(me_ref, g_ref, core_ref, chip_ref, xg_ref):
    planes = g_ref.shape[0]
    for ref, place in sides(me_ref, core_ref, chip_ref, planes):
        write_shifted(xg_ref, place(0, 1), ref[2])
    for p in range(planes):
        write_shifted(xg_ref, p + 1, g_ref[p])


def transposed_kernel(xg_ref, gt_ref):
    planes, _, channels, _ = gt_ref.shape
    height, width = xg_ref.shape[1] - 2, xg_ref.shape[2]

    def transposed(p, _):
        for b in range(3):
            for c in range(3):
                block = xg_ref[p, b : b + height, :, c * channels : (c + 1) * channels]
                gt_ref[p, b * 3 + c] = block.reshape(height * width, channels).T
        return 0

    lax.fori_loop(0, planes, transposed, 0)


def copy_all(moves, sems):
    copies = [
        pltpu.make_async_copy(source, target, sems.at[at])
        for at, (source, target) in enumerate(moves)
    ]
    for copy in copies:
        copy.start()
    for copy in copies:
        copy.wait()


def load_kernel(f_hbm, g_hbm, f_ref, g_ref, sems):
    copy_all(((f_hbm, f_ref), (g_hbm, g_ref)), sems)


def first_load_kernel(me_ref, f_hbm, g_hbm, first_hbm, second_hbm, *refs):
    shards_ref, core_ref, chip_ref, sems = refs
    planes = f_hbm.shape[0]
    odd = me_ref[0] % 2
    moves = [(first_hbm, shards_ref.at[0]), (second_hbm, shards_ref.at[1])]
    for ref, low in ((chip_ref, odd == 0), (core_ref, odd == 1)):
        moves.append((f_hbm.at[pl.ds(jnp.where(low, 0, planes - 2), 2)], ref.at[pl.ds(0, 2)]))
        moves.append((g_hbm.at[pl.ds(jnp.where(low, 0, planes - 1), 1)], ref.at[pl.ds(2, 1)]))
    copy_all(moves, sems)


def from_hbm(kernel, name, outs, args, scalars=(), wait_for=()):
    args = [pltpu.with_memory_space_constraint(a, pltpu.HBM) for a in args]
    first, last = len(scalars) + len(args), len(scalars) + len(args) + len(wait_for)

    def body(*refs):
        kernel(*refs[:first], *refs[last:])

    spaces = [pltpu.SMEM] * len(scalars) + [pltpu.HBM] * len(args) + [pl.ANY] * len(wait_for)
    return pl.pallas_call(
        body,
        out_shape=outs,
        in_specs=[pl.BlockSpec(memory_space=space) for space in spaces],
        out_specs=[pl.BlockSpec(memory_space=pltpu.VMEM) for _ in outs],
        scratch_shapes=[pltpu.SemaphoreType.DMA((6,))],
        name=name,
        compiler_params=pltpu.CompilerParams(vmem_limit_bytes=LIMIT),
        cost_estimate=pl.CostEstimate(flops=1000, bytes_accessed=0, transcendentals=0),
    )(*scalars, *args, *wait_for)


def join_kernel(*refs):
    *parts, out_ref = refs
    at = 0
    for part in parts:
        if len(part.shape) == 2:
            out_ref[at] = part[...]
            at += 1
        else:
            out_ref[at : at + part.shape[0]] = part[...]
            at += part.shape[0]


def window(ref, first, planes):
    height, width, lanes = ref.shape[1] - 2, ref.shape[2], ref.shape[3]
    return jnp.concatenate(
        [
            ref[first : first + planes, b : b + height].reshape(planes * height * width, lanes)
            for b in range(3)
        ],
        axis=1,
    )


def conv_rows(ref, first, planes, weight_ref):
    depth = weight_ref.shape[0] // 3
    cells = (ref.shape[1] - 2) * ref.shape[2]
    taps = [weight_ref[a * depth : (a + 1) * depth] for a in range(3)]

    def term(at, count, weight):
        return jnp.dot(window(ref, first + at, count), weight, preferred_element_type=F32)

    if planes == 1:
        return sum(term(a, 1, taps[a]) for a in range(3))
    channels = taps[0].shape[1]
    middle = term(1, planes - 1, jnp.concatenate(taps[:2], axis=1))
    late = jnp.dot(
        jnp.concatenate(
            [window(ref, first + 2, planes - 2), window(ref, first + planes + 1, 1)], axis=0
        ),
        taps[2],
        preferred_element_type=F32,
    )
    ends = (term(0, 1, taps[0]), late[(planes - 2) * cells :])
    last = term(planes, 1, jnp.concatenate(taps[1:], axis=1))
    parts = [[] for _ in range(planes)]
    parts[0].append(ends[0])
    for p in range(1, planes):
        rows = slice((p - 1) * cells, p * cells)
        parts[p].append(middle[rows, :channels])
        parts[p - 1].append(middle[rows, channels:])
    for p in range(2, planes):
        parts[p - 2].append(late[(p - 2) * cells : (p - 1) * cells])
    parts[planes - 1].append(last[:, :channels])
    parts[planes - 2].append(last[:, channels:])
    parts[planes - 1].append(ends[1])
    return jnp.concatenate([sum(terms[1:], terms[0]) for terms in parts], axis=0)


def near_far(core):
    return jnp.where(core == 0, 4, 2), jnp.where(core == 0, 2, 4)


def assemble(bank, me, pieces, dst):
    rows = pieces[0].shape[1]
    near, far = near_far(me % 2)
    starts = (me, me ^ 8, me ^ far, me ^ 8 ^ far)
    starts += tuple(start ^ 1 for start in (me, me ^ 8, me ^ near, me ^ 8 ^ near))
    for at, (piece, start) in enumerate(zip(pieces, starts)):
        for next_to, owner in enumerate((start, start ^ (near if at < 4 else far))):
            dst[pl.ds(pl.multiple_of(owner * rows, 8), rows)] = piece[2 * next_to + bank]


def assemble_in_order(bank, me, pieces, dst):
    dst[...] = pieces[bank][...]


def split_terms(me, total_ref, send_ref, keep_ref):
    count, rows, _ = keep_ref.shape
    core = me % 2
    for k in range(count):
        own = pl.multiple_of((2 * k + core) * rows, 8)
        other = pl.multiple_of((2 * k + 1 - core) * rows, 8)
        keep_ref[k] = total_ref[pl.ds(own, rows)]
        send_ref[k] = total_ref[pl.ds(other, rows)].astype(BF16)


def first_kernel(pieces, place, me_ref, *refs):
    piece_refs, (xf_ref, xg_ref, *out_refs) = refs[:pieces], refs[pieces:]
    bank_ref, hidden_ref, slope_ref, send_ref, keep_ref, total_ref = out_refs
    me = me_ref[0]
    planes, height, width, channels = hidden_ref.shape
    place(0, me, piece_refs, bank_ref)
    active, slope = gelu_parts(conv_rows(xf_ref, 1, planes, bank_ref))
    slope_ref[...] = slope.T
    hidden = active.astype(BF16)
    hidden_ref[...] = hidden.reshape(hidden_ref.shape)
    flipped = hidden.T
    for a in range(3):
        out = jnp.dot(flipped, window(xg_ref, 2 - a, planes), preferred_element_type=F32)
        for rest in range(9):
            tap, source = a * 9 + rest, 8 - rest
            total_ref[tap * channels : (tap + 1) * channels] = out[
                :, source * channels : (source + 1) * channels
            ]
    split_terms(me, total_ref, send_ref, keep_ref)


def second_kernel(pieces, place, me_ref, *refs):
    piece_refs, (xf_ref, gt_ref, slope_ref, *out_refs) = refs[:pieces], refs[pieces:]
    bank_ref, send_ref, keep_ref, total_ref = out_refs
    me = me_ref[0]
    channels = slope_ref.shape[0]
    planes, _, _, cells = gt_ref.shape
    planes -= 2
    place(1, me, piece_refs, bank_ref)
    back = jnp.concatenate(
        [bank_ref[tap * channels : (tap + 1) * channels] for tap in reversed(range(27))], axis=1
    )
    grads = []
    for z in range(planes):
        grad_hidden = jnp.dot(
            back, gt_ref[z : z + 3].reshape(27 * channels, cells), preferred_element_type=F32
        )
        grads.append((grad_hidden * slope_ref[:, z * cells : (z + 1) * cells]).astype(BF16))
    grad_pre = jnp.concatenate(grads, axis=1)
    for a in range(3):
        out = jnp.dot(grad_pre, window(xf_ref, 1 + a, planes), preferred_element_type=F32)
        for rest in range(9):
            tap = a * 9 + rest
            total_ref[tap * channels : (tap + 1) * channels] = out[
                :, rest * channels : (rest + 1) * channels
            ].T
    split_terms(me, total_ref, send_ref, keep_ref)


def hidden_kernel(count, me_ref, xf_ref, bank_ref, hidden_ref, xh_ref):
    me = me_ref[0]
    planes, height, width, channels = hidden_ref.shape
    for at, first, inside in ((0, 0, me > 0), (planes + 1, planes + 1, me < count - 1)):
        active, _ = gelu_parts(conv_rows(xf_ref, first, 1, bank_ref))
        active = jnp.where(inside, active, 0.0)
        write_shifted(xh_ref, at, active.astype(BF16).reshape(height, width, channels))
    for p in range(planes):
        write_shifted(xh_ref, p + 1, hidden_ref[p])


def output_kernel(xh_ref, second_ref, out_ref):
    out = conv_rows(xh_ref, 0, out_ref.shape[0], second_ref)
    out_ref[...] = out.astype(BF16).reshape(out_ref.shape)


def scatter_bits(me):
    low = me % 2 == 0
    y, z = (me // 2) % 2, (me // 4) % 2
    return low, jnp.where(low, y, z), jnp.where(low, z, y), me // 8


def sum_pair_kernel(me_ref, *refs):
    keep_refs, got_refs, (far_send, send, far_own, own) = refs[:2], refs[2:4], refs[4:]
    low, first, _, last = scatter_bits(me_ref[0])
    for bank, (keep_ref, got_ref) in enumerate(zip(keep_refs, got_refs)):
        for second in range(2):
            at = 2 * bank + second
            for side, send_ref, own_ref in ((1 - last, far_send, far_own), (last, send, own)):

                def total(bit):
                    k = 4 * side + jnp.where(low, 2 * second + bit, 2 * bit + second)
                    return keep_ref[k] + got_ref[k].astype(F32)

                own_ref[at] = total(first)
                send_ref[at] = total(1 - first).astype(BF16)


def sum_near_kernel(me_ref, own_ref, got_ref, send_ref, keep_ref):
    _, _, second, _ = scatter_bits(me_ref[0])
    for bank in range(2):
        mine, other = 2 * bank + second, 2 * bank + 1 - second
        keep_ref[bank] = own_ref[mine] + got_ref[mine].astype(F32)
        send_ref[bank] = (own_ref[other] + got_ref[other].astype(F32)).astype(BF16)


def sum_far_kernel(keep_ref, got_ref, send_ref):
    send_ref[...] = (keep_ref[...] + got_ref[...].astype(F32)).astype(BF16)


def sum_last_kernel(keep_ref, near_ref, far_ref, first_ref, second_ref):
    for bank, ref in enumerate((first_ref, second_ref)):
        ref[...] = keep_ref[bank] + near_ref[bank].astype(F32) + far_ref[bank].astype(F32)


def swap(value, count, distance):
    return lax.ppermute(value, "slab", [(i, i ^ distance) for i in range(count)])


def swap_mixed(value, count, even, odd):
    pairs = [(i, i ^ (odd if i % 2 else even)) for i in range(count)]
    return lax.ppermute(value, "slab", pairs)


def joined(parts, name, wait_for=()):
    depth = sum(part.shape[0] if part.ndim == 3 else 1 for part in parts)
    out = like((depth, *parts[0].shape[-2:]), BF16)
    return local_call(join_kernel, name, [out], parts, wait_for=wait_for)[0]


def shards(count, features, filters_first, filters_second, cotangent):
    planes, height, width, channels = features.shape
    cells = planes * height * width
    rows = filters_first.shape[0]
    taps = 27 * channels
    direct = count == 16 and rows % 8 == 0
    me = lax.axis_index("slab").astype(jnp.int32).reshape(1)
    shard_rows = rows if direct else taps // 16
    place = me if direct else jnp.zeros((1,), jnp.int32)
    order = assemble if direct else assemble_in_order

    edge = like((3, height, width, channels), BF16)
    own, to_core, to_chip = from_hbm(
        first_load_kernel,
        "load_shards_and_edges",
        [like((2, rows, channels), BF16), edge, edge],
        [features, cotangent, filters_first, filters_second],
        [me],
    )
    features, cotangent = from_hbm(
        load_kernel,
        "load",
        [like(features.shape, BF16), like(cotangent.shape, BF16)],
        [features, cotangent],
        wait_for=[to_chip],
    )
    from_core = swap(to_core, count, 1)
    next_chip = [(i, i + 1 if i % 2 else i - 1) for i in range(1, count - 1)]
    from_chip = lax.ppermute(to_chip, "slab", next_chip)
    edges = [from_core, from_chip]
    (xf,) = local_call(
        features_kernel,
        "feature_planes",
        [like((planes + 4, height + 2, width, 3 * channels), BF16)],
        [me, features, *edges],
        scalars=1,
    )
    wait_for = []
    if direct:
        far = swap(own, count, 8)
        near = swap_mixed(own, count, 4, 2)
        close = joined([own, near], "own_and_near", [])
        cross = swap_mixed(close, count, 2, 4)
        near = swap_mixed(far, count, 4, 2)
        away = joined([far, near], "far_and_near", [xf])
        cross_away = swap_mixed(away, count, 2, 4)
        wait_for = [cross, cross_away]
        pieces = [close, away, cross, cross_away]
    else:
        pieces = [
            lax.all_gather(shard, "slab", axis=0, tiled=True)
            for shard in (filters_first, filters_second)
        ]
    (xg,) = local_call(
        cotangent_kernel,
        "cotangent_planes",
        [like((planes + 2, height + 2, width, 3 * channels), BF16)],
        [me, cotangent, *edges],
        scalars=1,
        wait_for=wait_for[:1],
    )
    if direct:
        cross_sent = joined([cross], "cross", [xg])
        pieces += [swap(piece, count, 1) for piece in (close, away, cross_sent, cross_away)]
    (gt,) = local_call(
        transposed_kernel,
        "cotangent_windows",
        [like((planes + 2, 9, channels, height * width), BF16)],
        [xg],
        wait_for=wait_for[1:],
    )
    terms = [like((8, shard_rows, channels), BF16), like((8, shard_rows, channels), F32)]
    total = pltpu.VMEM((taps, channels), F32)
    bank, hidden, slope, send_second, keep_second = local_call(
        functools.partial(first_kernel, len(pieces), order),
        "hidden_and_second_grad",
        [
            like((taps, channels), BF16),
            like(features.shape, BF16),
            like((channels, cells), F32),
            *terms,
        ],
        [place, *pieces, xf, xg],
        scratch=[total],
        scalars=1,
        wait_for=[gt],
    )
    bank_second, send_first, keep_first = local_call(
        functools.partial(second_kernel, len(pieces), order),
        "first_grad",
        [like((taps, channels), BF16), *terms],
        [place, *pieces, xf, gt, slope],
        scratch=[total],
        scalars=1,
    )
    wait_for = [keep_first]
    if direct:
        got_second = swap(send_second, count, 1)
        wait_for.append(got_second)
    (xh,) = local_call(
        functools.partial(hidden_kernel, count),
        "hidden_planes",
        [like((planes + 2, height + 2, width, 3 * channels), BF16)],
        [me, xf, bank, hidden],
        scalars=1,
        wait_for=wait_for,
    )
    wait_for = []
    if direct:
        blocks = [like((4, rows, channels), BF16)] * 2 + [like((4, rows, channels), F32)] * 2
        far_send, send, far_own, own = local_call(
            sum_pair_kernel,
            "sum_pair",
            blocks,
            [
                me,
                keep_first,
                keep_second,
                swap(send_first, count, 1),
                got_second,
            ],
            scalars=1,
            wait_for=[xh],
        )
        halves = [like((2, rows, channels), BF16), like((2, rows, channels), F32)]
        far_got = swap_mixed(far_send, count, 2, 4)
        far_send, far_keep = local_call(
            sum_near_kernel, "far_near", halves, [me, far_own, far_got], scalars=1
        )
        far_got = swap_mixed(far_send, count, 4, 2)
        got = swap_mixed(send, count, 2, 4)
        send, keep = local_call(
            sum_near_kernel, "own_near", halves, [me, own, got], scalars=1, wait_for=[far_send]
        )
        got = swap_mixed(send, count, 4, 2)
        (far_send,) = local_call(
            sum_far_kernel, "far_last", halves[:1], [far_keep, far_got]
        )
        far_got = swap(far_send, count, 8)
        wait_for = [far_send]
    (output,) = local_call(
        output_kernel, "output_conv", [like(features.shape, BF16)], [xh, bank_second], wait_for=wait_for
    )
    if direct:
        out = like((rows, channels), F32)
        grad_first, grad_second = local_call(
            sum_last_kernel, "sum_last", [out, out], [keep, got, far_got]
        )
    else:
        grad_first, grad_second = (
            lax.psum_scatter(
                jnp.stack([keep, send.astype(F32)], 1).reshape(taps, channels),
                "slab",
                scatter_dimension=0,
                tiled=True,
            )
            for send, keep in ((send_first, keep_first), (send_second, keep_second))
        )
    return (output, grad_first, grad_second)


def solution(mesh):
    return jax.shard_map(
        functools.partial(shards, mesh.shape["slab"]),
        mesh=mesh,
        in_specs=(
            P(("groups", "slab"), None, None, None),
            P("slab", None),
            P("slab", None),
            P(("groups", "slab"), None, None, None),
        ),
        out_specs=(
            P(("groups", "slab"), None, None, None),
            P(("groups", "slab"), None),
            P(("groups", "slab"), None),
        ),
        check_vma=False,
    )
```

```python
import functools

import jax
import jax.numpy as jnp
from jax import lax
from jax.experimental import pallas as pl
from jax.experimental.pallas import tpu as pltpu
from jax.sharding import PartitionSpec as P

inv_root_two = 0.7071067811865476
inv_root_two_pi = 0.3989422804014327

BF16 = jnp.bfloat16
F32 = jnp.float32
LIMIT = 14 << 20


def gelu_parts(value):
    normal_cdf = 0.5 * (1.0 + lax.erf(value * inv_root_two))
    slope = normal_cdf + value * jnp.exp(-0.5 * value * value) * inv_root_two_pi
    return (value * normal_cdf, slope)


def local_call(kernel, name, outs, args, scratch=(), scalars=0, wait_for=()):
    first, last = len(args), len(args) + len(wait_for)

    def body(*refs):
        kernel(*refs[:first], *refs[last:])

    spaces = [pltpu.SMEM] * scalars + [pltpu.VMEM] * (first - scalars) + [pl.ANY] * len(wait_for)
    return pl.pallas_call(
        body,
        out_shape=list(outs),
        in_specs=[pl.BlockSpec(memory_space=space) for space in spaces],
        out_specs=[pl.BlockSpec(memory_space=pltpu.VMEM) for _ in outs],
        scratch_shapes=list(scratch),
        name=name,
        compiler_params=pltpu.CompilerParams(vmem_limit_bytes=LIMIT),
        cost_estimate=pl.CostEstimate(flops=1000, bytes_accessed=0, transcendentals=0),
    )(*args, *wait_for)


def like(shape, dtype):
    return jax.ShapeDtypeStruct(shape, dtype)


def write_shifted(dst, at, plane):
    height, width, channels = plane.shape
    flat = plane.astype(F32).reshape(height * width, channels)
    column = lax.broadcasted_iota(jnp.int32, flat.shape, 0) % width
    left = jnp.where(column == 0, 0.0, pltpu.roll(flat, 1, 0))
    right = jnp.where(column == width - 1, 0.0, pltpu.roll(flat, height * width - 1, 0))
    row = jnp.zeros((1, width, 3 * channels), BF16)
    dst[at, 0:1] = row
    dst[at, height + 1 : height + 2] = row
    for block, value in enumerate((left, flat, right)):
        dst[at, 1 : height + 1, :, block * channels : (block + 1) * channels] = (
            value.astype(BF16).reshape(height, width, channels)
        )


def sides(me_ref, core_ref, chip_ref, own):
    odd = me_ref[0] % 2
    for ref, below in ((core_ref, odd == 1), (chip_ref, odd == 0)):
        yield ref, lambda p, count: jnp.where(below, p, own + count + p)


def features_kernel(me_ref, f_ref, core_ref, chip_ref, xf_ref):
    planes = f_ref.shape[0]
    for ref, place in sides(me_ref, core_ref, chip_ref, planes):
        for p in range(2):
            write_shifted(xf_ref, place(p, 2), ref[p])
    for p in range(planes):
        write_shifted(xf_ref, p + 2, f_ref[p])


def cotangent_kernel(me_ref, g_ref, core_ref, chip_ref, xg_ref, gt_ref):
    planes, height, width, channels = g_ref.shape
    for ref, place in sides(me_ref, core_ref, chip_ref, planes):
        write_shifted(xg_ref, place(0, 1), ref[2])
    for p in range(planes):
        write_shifted(xg_ref, p + 1, g_ref[p])

    def transposed(p, _):
        for b in range(3):
            for c in range(3):
                block = xg_ref[p, b : b + height, :, c * channels : (c + 1) * channels]
                gt_ref[p, b * 3 + c] = block.reshape(height * width, channels).T
        return 0

    lax.fori_loop(0, planes + 2, transposed, 0)


def copy_all(moves, sems):
    copies = [
        pltpu.make_async_copy(source, target, sems.at[at])
        for at, (source, target) in enumerate(moves)
    ]
    for copy in copies:
        copy.start()
    for copy in copies:
        copy.wait()


def load_kernel(f_hbm, g_hbm, f_ref, g_ref, sems):
    copy_all(((f_hbm, f_ref), (g_hbm, g_ref)), sems)


def first_load_kernel(me_ref, f_hbm, g_hbm, first_hbm, second_hbm, *refs):
    shards_ref, core_ref, chip_ref, sems = refs
    planes = f_hbm.shape[0]
    odd = me_ref[0] % 2
    moves = [(first_hbm, shards_ref.at[0]), (second_hbm, shards_ref.at[1])]
    for ref, low in ((chip_ref, odd == 0), (core_ref, odd == 1)):
        moves.append((f_hbm.at[pl.ds(jnp.where(low, 0, planes - 2), 2)], ref.at[pl.ds(0, 2)]))
        moves.append((g_hbm.at[pl.ds(jnp.where(low, 0, planes - 1), 1)], ref.at[pl.ds(2, 1)]))
    copy_all(moves, sems)


def from_hbm(kernel, name, outs, args, scalars=(), wait_for=()):
    args = [pltpu.with_memory_space_constraint(a, pltpu.HBM) for a in args]
    first, last = len(scalars) + len(args), len(scalars) + len(args) + len(wait_for)

    def body(*refs):
        kernel(*refs[:first], *refs[last:])

    spaces = [pltpu.SMEM] * len(scalars) + [pltpu.HBM] * len(args) + [pl.ANY] * len(wait_for)
    return pl.pallas_call(
        body,
        out_shape=outs,
        in_specs=[pl.BlockSpec(memory_space=space) for space in spaces],
        out_specs=[pl.BlockSpec(memory_space=pltpu.VMEM) for _ in outs],
        scratch_shapes=[pltpu.SemaphoreType.DMA((6,))],
        name=name,
        compiler_params=pltpu.CompilerParams(vmem_limit_bytes=LIMIT),
        cost_estimate=pl.CostEstimate(flops=1000, bytes_accessed=0, transcendentals=0),
    )(*scalars, *args, *wait_for)


def join_kernel(*refs):
    *parts, out_ref = refs
    at = 0
    for part in parts:
        if len(part.shape) == 2:
            out_ref[at] = part[...]
            at += 1
        else:
            out_ref[at : at + part.shape[0]] = part[...]
            at += part.shape[0]


def window(ref, first, planes):
    height, width, lanes = ref.shape[1] - 2, ref.shape[2], ref.shape[3]
    return jnp.concatenate(
        [
            ref[first : first + planes, b : b + height].reshape(planes * height * width, lanes)
            for b in range(3)
        ],
        axis=1,
    )


def conv_rows(ref, first, planes, weight_ref):
    depth = weight_ref.shape[0] // 3
    cells = (ref.shape[1] - 2) * ref.shape[2]
    taps = [weight_ref[a * depth : (a + 1) * depth] for a in range(3)]

    def term(at, count, weight):
        return jnp.dot(window(ref, first + at, count), weight, preferred_element_type=F32)

    if planes == 1:
        return sum(term(a, 1, taps[a]) for a in range(3))
    channels = taps[0].shape[1]
    middle = term(1, planes - 1, jnp.concatenate(taps[:2], axis=1))
    late = term(2, planes - 2, taps[2])
    ends = (term(0, 1, taps[0]), term(planes + 1, 1, taps[2]))
    last = term(planes, 1, jnp.concatenate(taps[1:], axis=1))
    parts = [[] for _ in range(planes)]
    parts[0].append(ends[0])
    for p in range(1, planes):
        rows = slice((p - 1) * cells, p * cells)
        parts[p].append(middle[rows, :channels])
        parts[p - 1].append(middle[rows, channels:])
    for p in range(2, planes):
        parts[p - 2].append(late[(p - 2) * cells : (p - 1) * cells])
    parts[planes - 1].append(last[:, :channels])
    parts[planes - 2].append(last[:, channels:])
    parts[planes - 1].append(ends[1])
    return jnp.concatenate([sum(terms[1:], terms[0]) for terms in parts], axis=0)


def near_far(core):
    return jnp.where(core == 0, 4, 2), jnp.where(core == 0, 2, 4)


def assemble(bank, me, pieces, dst):
    rows = pieces[0].shape[1]
    near, far = near_far(me % 2)
    starts = (me, me ^ 8, me ^ far, me ^ 8 ^ far)
    starts += tuple(start ^ 1 for start in (me, me ^ 8, me ^ near, me ^ 8 ^ near))
    for at, (piece, start) in enumerate(zip(pieces, starts)):
        for next_to, owner in enumerate((start, start ^ (near if at < 4 else far))):
            dst[pl.ds(pl.multiple_of(owner * rows, 8), rows)] = piece[2 * next_to + bank]


def assemble_in_order(bank, me, pieces, dst):
    dst[...] = pieces[bank][...]


def split_terms(me, total_ref, send_ref, keep_ref):
    count, rows, _ = keep_ref.shape
    core = me % 2
    for k in range(count):
        own = pl.multiple_of((2 * k + core) * rows, 8)
        other = pl.multiple_of((2 * k + 1 - core) * rows, 8)
        keep_ref[k] = total_ref[pl.ds(own, rows)]
        send_ref[k] = total_ref[pl.ds(other, rows)].astype(BF16)


def first_kernel(pieces, place, me_ref, *refs):
    piece_refs, (xf_ref, xg_ref, *out_refs) = refs[:pieces], refs[pieces:]
    bank_ref, hidden_ref, slope_ref, send_ref, keep_ref, total_ref = out_refs
    me = me_ref[0]
    planes, height, width, channels = hidden_ref.shape
    place(0, me, piece_refs, bank_ref)
    active, slope = gelu_parts(conv_rows(xf_ref, 1, planes, bank_ref))
    slope_ref[...] = slope.T
    hidden = active.astype(BF16)
    hidden_ref[...] = hidden.reshape(hidden_ref.shape)
    flipped = hidden.T
    for a in range(3):
        out = jnp.dot(flipped, window(xg_ref, 2 - a, planes), preferred_element_type=F32)
        for rest in range(9):
            tap, source = a * 9 + rest, 8 - rest
            total_ref[tap * channels : (tap + 1) * channels] = out[
                :, source * channels : (source + 1) * channels
            ]
    split_terms(me, total_ref, send_ref, keep_ref)


def second_kernel(pieces, place, me_ref, *refs):
    piece_refs, (xf_ref, gt_ref, slope_ref, *out_refs) = refs[:pieces], refs[pieces:]
    bank_ref, send_ref, keep_ref, total_ref = out_refs
    me = me_ref[0]
    channels = slope_ref.shape[0]
    planes, _, _, cells = gt_ref.shape
    planes -= 2
    place(1, me, piece_refs, bank_ref)
    back = jnp.concatenate(
        [bank_ref[tap * channels : (tap + 1) * channels] for tap in reversed(range(27))], axis=1
    )
    grads = []
    for z in range(planes):
        grad_hidden = jnp.dot(
            back, gt_ref[z : z + 3].reshape(27 * channels, cells), preferred_element_type=F32
        )
        grads.append((grad_hidden * slope_ref[:, z * cells : (z + 1) * cells]).astype(BF16))
    grad_pre = jnp.concatenate(grads, axis=1)
    for a in range(3):
        out = jnp.dot(grad_pre, window(xf_ref, 1 + a, planes), preferred_element_type=F32)
        for rest in range(9):
            tap = a * 9 + rest
            total_ref[tap * channels : (tap + 1) * channels] = out[
                :, rest * channels : (rest + 1) * channels
            ].T
    split_terms(me, total_ref, send_ref, keep_ref)


def hidden_kernel(count, me_ref, xf_ref, bank_ref, hidden_ref, xh_ref):
    me = me_ref[0]
    planes, height, width, channels = hidden_ref.shape
    for at, first, inside in ((0, 0, me > 0), (planes + 1, planes + 1, me < count - 1)):
        active, _ = gelu_parts(conv_rows(xf_ref, first, 1, bank_ref))
        active = jnp.where(inside, active, 0.0)
        write_shifted(xh_ref, at, active.astype(BF16).reshape(height, width, channels))
    for p in range(planes):
        write_shifted(xh_ref, p + 1, hidden_ref[p])


def output_kernel(xh_ref, second_ref, out_ref):
    out = conv_rows(xh_ref, 0, out_ref.shape[0], second_ref)
    out_ref[...] = out.astype(BF16).reshape(out_ref.shape)


def scatter_bits(me):
    low = me % 2 == 0
    y, z = (me // 2) % 2, (me // 4) % 2
    return low, jnp.where(low, y, z), jnp.where(low, z, y), me // 8


def sum_pair_kernel(me_ref, keep_ref, got_ref, *refs):
    before, (far_send, far_own, send, own) = refs[:-4], refs[-4:]
    low, first, _, last = scatter_bits(me_ref[0])
    if before:
        for ref, earlier in zip((send, own), before):
            ref[2:4] = earlier[...]
    for second in range(2):
        for side, send_ref, own_ref in ((1 - last, far_send, far_own), (last, send, own)):

            def total(bit):
                k = 4 * side + jnp.where(low, 2 * second + bit, 2 * bit + second)
                return keep_ref[k] + got_ref[k].astype(F32)

            own_ref[second] = total(first)
            send_ref[second] = total(1 - first).astype(BF16)


def sum_near_kernel(me_ref, own_ref, got_ref, *refs):
    before, (send_ref, keep_ref) = refs[:-2], refs[-2:]
    _, _, second, _ = scatter_bits(me_ref[0])
    for bank in range(own_ref.shape[0] // 2):
        mine, other = 2 * bank + second, 2 * bank + 1 - second
        keep_ref[bank] = own_ref[mine] + got_ref[mine].astype(F32)
        send_ref[bank] = (own_ref[other] + got_ref[other].astype(F32)).astype(BF16)
    for ref, earlier in zip((send_ref, keep_ref), before):
        ref[1:2] = earlier[...]


def sum_far_kernel(keep_ref, got_ref, send_ref):
    send_ref[...] = (keep_ref[...] + got_ref[...].astype(F32)).astype(BF16)


def sum_back_kernel(keep_ref, far_ref, out_ref):
    out_ref[...] = keep_ref[...] + far_ref[...].astype(F32)


def sum_last_kernel(keep_ref, near_ref, first_ref, second_ref):
    for bank, ref in enumerate((first_ref, second_ref)):
        ref[...] = keep_ref[bank] + near_ref[bank].astype(F32)


def swap(value, count, distance):
    return lax.ppermute(value, "slab", [(i, i ^ distance) for i in range(count)])


def swap_mixed(value, count, even, odd):
    pairs = [(i, i ^ (odd if i % 2 else even)) for i in range(count)]
    return lax.ppermute(value, "slab", pairs)


def joined(parts, name, wait_for=()):
    depth = sum(part.shape[0] if part.ndim == 3 else 1 for part in parts)
    out = like((depth, *parts[0].shape[-2:]), BF16)
    return local_call(join_kernel, name, [out], parts, wait_for=wait_for)[0]


def shards(count, features, filters_first, filters_second, cotangent):
    planes, height, width, channels = features.shape
    cells = planes * height * width
    rows = filters_first.shape[0]
    taps = 27 * channels
    direct = count == 16 and rows % 8 == 0
    me = lax.axis_index("slab").astype(jnp.int32).reshape(1)
    shard_rows = rows if direct else taps // 16
    place = me if direct else jnp.zeros((1,), jnp.int32)
    order = assemble if direct else assemble_in_order

    edge = like((3, height, width, channels), BF16)
    own, to_core, to_chip = from_hbm(
        first_load_kernel,
        "load_shards_and_edges",
        [like((2, rows, channels), BF16), edge, edge],
        [features, cotangent, filters_first, filters_second],
        [me],
    )
    features, cotangent = from_hbm(
        load_kernel,
        "load",
        [like(features.shape, BF16), like(cotangent.shape, BF16)],
        [features, cotangent],
        wait_for=[to_chip],
    )
    from_core = swap(to_core, count, 1)
    next_chip = [(i, i + 1 if i % 2 else i - 1) for i in range(1, count - 1)]
    from_chip = lax.ppermute(to_chip, "slab", next_chip)
    edges = [from_core, from_chip]
    (xf,) = local_call(
        features_kernel,
        "feature_planes",
        [like((planes + 4, height + 2, width, 3 * channels), BF16)],
        [me, features, *edges],
        scalars=1,
    )
    wait_for = []
    if direct:
        far = swap(own, count, 8)
        near = swap_mixed(own, count, 4, 2)
        close = joined([own, near], "own_and_near", [])
        cross = swap_mixed(close, count, 2, 4)
        near = swap_mixed(far, count, 4, 2)
        away = joined([far, near], "far_and_near", [xf])
        cross_away = swap_mixed(away, count, 2, 4)
        wait_for = [cross_away]
        pieces = [close, away, cross, cross_away]
        pieces += [swap(piece, count, 1) for piece in pieces]
    else:
        pieces = [
            lax.all_gather(shard, "slab", axis=0, tiled=True)
            for shard in (filters_first, filters_second)
        ]
    xg, gt = local_call(
        cotangent_kernel,
        "cotangent_planes",
        [
            like((planes + 2, height + 2, width, 3 * channels), BF16),
            like((planes + 2, 9, channels, height * width), BF16),
        ],
        [me, cotangent, *edges],
        scalars=1,
        wait_for=wait_for,
    )
    terms = [like((8, shard_rows, channels), BF16), like((8, shard_rows, channels), F32)]
    total = pltpu.VMEM((taps, channels), F32)
    bank, hidden, slope, send_second, keep_second = local_call(
        functools.partial(first_kernel, len(pieces), order),
        "hidden_and_second_grad",
        [
            like((taps, channels), BF16),
            like(features.shape, BF16),
            like((channels, cells), F32),
            *terms,
        ],
        [place, *pieces, xf, xg],
        scratch=[total],
        scalars=1,
    )
    bank_second, send_first, keep_first = local_call(
        functools.partial(second_kernel, len(pieces), order),
        "first_grad",
        [like((taps, channels), BF16), *terms],
        [place, *pieces, xf, gt, slope],
        scratch=[total],
        scalars=1,
    )
    def both(count):
        return [like((count, rows, channels), BF16), like((count, rows, channels), F32)]

    wait_for = [keep_first]
    if direct:
        far_send, far_own_second, *own_second = local_call(
            sum_pair_kernel,
            "second_pair",
            both(2) + both(2),
            [me, keep_second, swap(send_second, count, 1)],
            scalars=1,
        )
        far_got_second = swap_mixed(far_send, count, 2, 4)
        wait_for.append(far_send)
    (xh,) = local_call(
        functools.partial(hidden_kernel, count),
        "hidden_planes",
        [like((planes + 2, height + 2, width, 3 * channels), BF16)],
        [me, xf, bank, hidden],
        scalars=1,
        wait_for=wait_for,
    )
    wait_for = []
    if direct:
        far_send, far_own, send, own = local_call(
            sum_pair_kernel,
            "first_pair",
            both(2) + both(4),
            [me, keep_first, swap(send_first, count, 1), *own_second],
            scalars=1,
            wait_for=[xh],
        )
        far_got = swap_mixed(far_send, count, 2, 4)
        far_second = local_call(
            sum_near_kernel,
            "second_far_near",
            both(1),
            [me, far_own_second, far_got_second],
            scalars=1,
            wait_for=[far_send],
        )
        far_send, far_keep = local_call(
            sum_near_kernel, "first_far_near", both(2), [me, far_own, far_got, *far_second], scalars=1
        )
        far_got = swap_mixed(far_send, count, 4, 2)
        (far_send,) = local_call(sum_far_kernel, "far_last", both(2)[:1], [far_keep, far_got])
        far_got = swap(far_send, count, 8)
        got = swap_mixed(send, count, 2, 4)
        send, keep = local_call(
            sum_near_kernel, "own_near", both(2), [me, own, got], scalars=1, wait_for=[far_send]
        )
        got = swap_mixed(send, count, 4, 2)
        wait_for = [send]
    (output,) = local_call(
        output_kernel, "output_conv", [like(features.shape, BF16)], [xh, bank_second], wait_for=wait_for
    )
    if direct:
        (keep,) = local_call(sum_back_kernel, "far_back", both(2)[1:], [keep, far_got])
        out = like((rows, channels), F32)
        grad_first, grad_second = local_call(
            sum_last_kernel, "sum_last", [out, out], [keep, got]
        )
    else:
        grad_first, grad_second = (
            lax.psum_scatter(
                jnp.stack([keep, send.astype(F32)], 1).reshape(taps, channels),
                "slab",
                scatter_dimension=0,
                tiled=True,
            )
            for send, keep in ((send_first, keep_first), (send_second, keep_second))
        )
    return (output, grad_first, grad_second)


def solution(mesh):
    return jax.shard_map(
        functools.partial(shards, mesh.shape["slab"]),
        mesh=mesh,
        in_specs=(
            P(("groups", "slab"), None, None, None),
            P("slab", None),
            P("slab", None),
            P(("groups", "slab"), None, None, None),
        ),
        out_specs=(
            P(("groups", "slab"), None, None, None),
            P(("groups", "slab"), None),
            P(("groups", "slab"), None),
        ),
        check_vma=False,
    )
```
